128 devices in a mesh: group: 16 (over y, x), local: 8 (over z, core).
Axes of the slice: x: 4, y: 4, z: 4, core: 2. Of those that a mesh axis runs over, the one named last changes fastest.
Arguments:
- grad_out: bfloat16 [2048, 7168], P('group', 'local'), may hold values from -6 to 6
- combine_weight: float32 [2048, 8], P('group'), may hold values from 0.1 to 1
- token_groups: int32 [2048, 4], P('group'), may hold values from 0 to 15, all different within a row; in each aligned block of 128 rows (0 to 127, 128 to 255, ...) at most 64 rows name the same one
- expert_pick: int32 [2048, 8], P('group'), may hold values from 0 to 11, as said below
- saved_gate: bfloat16 [48, 1024, 1024], P('group', None, 'local'), may hold values from -6 to 6
- saved_up: bfloat16 [48, 1024, 1024], P('group', None, 'local'), may hold values from -6 to 6
- w_gate: bfloat16 [48, 7168, 1024], P('group', None, 'local'), may hold values from -0.25 to 0.25
- w_up: bfloat16 [48, 7168, 1024], P('group', None, 'local'), may hold values from -0.1875 to 0.1875
- w_down: bfloat16 [48, 1024, 7168], P('group', 'local'), may hold values from -0.0625 to 0.0625
Outputs:
- grad_in: bfloat16 [2048, 7168], P('group', 'local')
The draws below stay inside these ranges and needn't reach their ends.
Inputs may be any that keep to these rules, and one draw needn't show every extreme that they name: `token_groups`: each row names 4 different groups; within the rows of one index of group no group is named by more than 64 rows, a bound that some block reaches. `expert_pick`: each row names 8 different slots; slot v stands for expert v % 3 of the group token_groups[row, v // 3], and each of the row's 4 groups is named by at least one slot.
All inputs are finite; a program needn't handle non-finite values.
Results may differ from the reference program's by a relative error of at most 0.017.
Values may be sent and summed in bfloat16 or wider, within the bound.
No kernel may reach another device: no remote copies, remote signals or barrier semaphores. Data moves between devices by JAX's collectives and lax.ppermute only.
A program may use at most 128 MiB of HBM per device.

```python
import math
import jax
import jax.numpy as jnp
import numpy as np
from jax import lax

D = 7168
FF = 1024
EXP_GRP = 3
TOPK = 8
GRP_TOP = 4
TOK_GRP = 128
CAP = 64
ROWS_G = 1024
TOKENS = 2048
EXPERTS = 48
N_GROUP = 16
N_LOCAL = 8


def draw_expert_pick(key, part):
    key = jax.random.fold_in(key, 11)
    first_key, order_key = jax.random.split(key)
    mandatory = jax.random.randint(first_key, (TOKENS, GRP_TOP), 0, EXP_GRP).astype(jnp.int32)
    bases = jnp.arange(GRP_TOP, dtype=jnp.int32)[None, :] * EXP_GRP
    leading = bases + mandatory
    spare = jnp.concatenate([bases + (mandatory + shift_by) % EXP_GRP for shift_by in range(1, EXP_GRP)], axis=1)
    order_keys = jax.random.split(order_key, TOKENS)
    orders = jax.vmap(lambda one_key: jax.random.permutation(one_key, GRP_TOP * (EXP_GRP - 1)))(order_keys)
    extra = jnp.take_along_axis(spare, orders[:, :TOPK - GRP_TOP].astype(jnp.int32), axis=1)
    return jnp.concatenate([leading, extra], axis=1).astype(jnp.int32)


def raised(result, rng, source, target, blocks, factor):
    def block_of(position):
        return (jnp.arange(result.shape[position]) // (result.shape[position] // blocks)).reshape((-1,) + (1,) * (result.ndim - 1 - position))

    first = jax.random.permutation(rng, blocks)[block_of(target)]
    other_side = (block_of(target) + blocks // 2) % blocks
    return jnp.where((block_of(source) == first) | (block_of(source) == other_side), factor * result, result)


def shard_levels(rng, dims, pieces, least, top_value):
    def one(axis_at, blocks):
        draws = jax.random.uniform(jax.random.fold_in(jax.random.fold_in(rng, 6), axis_at), (blocks,), jnp.float32, least / len(pieces), top_value / len(pieces))
        return jnp.repeat(jnp.exp(draws), dims[axis_at] // blocks).reshape((-1,) + (1,) * (len(dims) - axis_at - 1))

    factor_of = one(*pieces[0])
    for cut in pieces[1:]:
        factor_of = factor_of * one(*cut)
    return factor_of


def shared_out(own_key, own, number, rows, amount, top, reach, slope):
    sequence = jax.random.permutation(own_key, amount)
    heavy_load, common = shares(amount, rows * top, reach, slope, True), shares(amount, rows * top, reach, slope, False)
    places = jnp.arange(amount)

    def named(lengths, rotation):
        used = int((lengths > 0).sum())
        fixed = max(1, used // 4)
        moved = fixed + (places - fixed + rotation * (used - fixed)) % max(1, amount - fixed)
        return jnp.zeros((amount,), jnp.int32).at[sequence[jnp.where(places < fixed, places, moved)]].set(jnp.asarray(lengths, jnp.int32))

    lengths = jnp.where(number % 4 == 0, named(heavy_load, number // 4), named(common, number - number // 4 - 1))
    mixed = jax.random.permutation(jax.random.fold_in(own, 3), amount)
    source_of, receiver = mixed[0:amount // 2 * 2:2], mixed[1:amount // 2 * 2:2]
    room = jnp.minimum(lengths[source_of] - 1, reach - lengths[receiver]) // 2
    room = jnp.where((source_of == sequence[0]) | (receiver == sequence[0]) | (lengths[receiver] == 0), 0, jnp.maximum(room, 0))
    moved = jax.random.randint(jax.random.fold_in(own, 4), (amount // 2,), 0, 1 << 20) % (room + 1)
    lengths = lengths.at[source_of].add(-moved).at[receiver].add(moved)
    items = jnp.searchsorted(jnp.cumsum(lengths), jnp.arange(rows * top), side="right").astype(jnp.int32)
    table = items.reshape(top, rows).T
    table = table[jax.random.permutation(jax.random.fold_in(own, 1), rows)]
    rotation = jax.random.randint(jax.random.fold_in(own, 2), (rows, 1), 0, top)
    return jnp.take_along_axis(table, (jnp.arange(top)[None, :] + rotation) % top, axis=1)


def shares(amount, total, most, skew, full):
    portions = [(1 << 20) // math.isqrt(grade ** skew) + 1 for grade in range(1, amount + 1)]
    largest = most if full else min(most, max(-(-total // amount), total * portions[0] // sum(portions)))
    least = 1 if total - largest >= amount - 1 else 0
    given, surplus = [largest] + [least] * (amount - 1), total - largest - least * (amount - 1)
    while surplus > 0:
        free = [i for i in range(1, amount) if given[i] < largest] or [i for i in range(1, amount) if given[i] < most]
        pool, remaining = sum([portions[i] for i in free]), surplus
        for i in free:
            more = min(most - given[i], max(1, remaining * portions[i] // pool), surplus)
            given[i] = given[i] + more
            surplus = surplus - more
    return np.array(given)


def scatter_about(stream_key, shape, scale, reach, pieces=(), kind=jnp.bfloat16):
    loudness = shard_levels(stream_key, shape, pieces, -0.22, 0.18) if pieces else 1.0
    values = jax.random.normal(stream_key, shape, jnp.float32) * scale * loudness
    return jnp.minimum(jnp.maximum(values, -reach), reach).astype(kind)


def heavy_noise(stream_key, dims, width, bound, cuts, heavy, kind=jnp.bfloat16):
    values = width * jax.random.normal(stream_key, dims, jnp.float32)
    if cuts:
        values = values * shard_levels(stream_key, dims, cuts, -0.22, 0.18)
    return jnp.clip(raised(values, jax.random.fold_in(stream_key, 3), *heavy), -bound, bound).astype(kind)


def setup_inputs(seed: int = 0) -> dict:
    streams_of = jax.random.split(jax.random.key(seed), 10)
    grad_out = scatter_about(streams_of[0], (TOKENS, D), 1.0, 6.0, ((0, 16), (1, 8)))
    combine_weight = jnp.clip(jnp.exp(math.log(1.0) - 2.3025851 * jax.random.uniform(streams_of[1], (TOKENS, TOPK), jnp.float32) ** shard_levels(streams_of[1], (TOKENS, TOPK), ((0, 16),), -0.2, 0.2)), 0.1, 1.0)
    token_groups_keys = jax.random.split(jax.random.fold_in(streams_of[2], 1), TOKENS // TOK_GRP)
    token_groups_turns = jax.random.permutation(jax.random.fold_in(streams_of[2], 3), TOKENS // TOK_GRP)
    token_groups = jax.vmap(lambda own, number: shared_out(jax.random.fold_in(streams_of[2], 2), own, number, TOK_GRP, N_GROUP, GRP_TOP, CAP, 2))(token_groups_keys, token_groups_turns).reshape((TOKENS, GRP_TOP))
    expert_pick = draw_expert_pick(jax.random.fold_in(streams_of[9], 71), 0)
    saved_gate = scatter_about(streams_of[4], (EXPERTS, ROWS_G, FF), 1.5, 6.0, ((0, 16), (2, 8)))
    saved_up = scatter_about(streams_of[5], (EXPERTS, ROWS_G, FF), 1.0, 6.0, ((0, 16), (2, 8)))
    w_gate = heavy_noise(streams_of[6], (EXPERTS, D, FF), FF ** -0.5, 0.25, ((0, 16), (2, 8)), (2, 1, 8, 2.0))
    w_up = scatter_about(streams_of[7], (EXPERTS, D, FF), FF ** -0.5, 0.1875, ((0, 16), (2, 8)))
    w_down = scatter_about(streams_of[8], (EXPERTS, FF, D), D ** -0.5, 0.0625, ((0, 16), (1, 8)))
    return {"grad_out": grad_out, "combine_weight": combine_weight, "token_groups": token_groups, "expert_pick": expert_pick, "saved_gate": saved_gate, "saved_up": saved_up, "w_gate": w_gate, "w_up": w_up, "w_down": w_down}


def dispatch_tables(token_groups, expert_pick, combine_weight, group_count, slot_count):
    group_ids = jnp.arange(group_count, dtype=jnp.int32)
    member = jnp.any(token_groups[:, :, None] == group_ids[None, None, :], axis=1).astype(jnp.int32)
    slot_index = jnp.cumsum(member, axis=0) - member
    slot_ids = jnp.arange(slot_count, dtype=jnp.int32)
    routing_table = ((member.T[:, None, :] == 1) & (slot_index.T[:, None, :] == slot_ids[None, :, None])).astype(jnp.float32)
    chosen = jnp.take_along_axis(token_groups, (expert_pick // EXP_GRP).astype(jnp.int32), axis=1)
    within = expert_pick % EXP_GRP
    group_hot = (chosen[:, :, None] == group_ids[None, None, :]).astype(jnp.float32)
    expert_hot = (within[:, :, None] == jnp.arange(EXP_GRP, dtype=jnp.int32)[None, None, :]).astype(jnp.float32)
    spread = jnp.einsum("tk,tkg,tkj->tgj", combine_weight, group_hot, expert_hot, precision=lax.Precision.HIGHEST)
    lane_weights = jnp.einsum("gct,tgj->gcj", routing_table, spread, precision=lax.Precision.HIGHEST).astype(jnp.bfloat16)
    return routing_table, lane_weights


def expert_grads(hidden_grad, lane_cols, saved_gate, saved_up):
    scaled = hidden_grad * lane_cols
    gate_value = saved_gate.astype(jnp.float32)
    up_value = saved_up.astype(jnp.float32)
    sigmoid_gate = jax.nn.sigmoid(gate_value)
    grad_gate = (scaled * up_value * sigmoid_gate * (1.0 + gate_value * (1.0 - sigmoid_gate))).astype(jnp.bfloat16)
    grad_up = (scaled * gate_value * sigmoid_gate).astype(jnp.bfloat16)
    return grad_gate, grad_up


def reference(grad_out, combine_weight, token_groups, expert_pick, saved_gate, saved_up, w_gate, w_up, w_down):
    token_blocks = grad_out.reshape(N_GROUP, TOK_GRP, D).astype(jnp.float32)
    tables, lanes = jax.vmap(lambda tg, ep, cw: dispatch_tables(tg, ep, cw, N_GROUP, CAP))(
        token_groups.reshape(N_GROUP, TOK_GRP, GRP_TOP),
        expert_pick.reshape(N_GROUP, TOK_GRP, TOPK),
        combine_weight.reshape(N_GROUP, TOK_GRP, TOPK))
    hidden_blk = FF // N_LOCAL

    def per_group(running, group_now):
        group_tables = lax.dynamic_index_in_dim(tables, group_now, 1, keepdims=False)
        dispatched = jnp.einsum("sct,std->scd", group_tables, token_blocks, precision=lax.Precision.HIGHEST)
        dispatched = dispatched.astype(jnp.bfloat16).reshape(ROWS_G, D).astype(jnp.float32)
        group_lanes = lax.dynamic_index_in_dim(lanes, group_now, 1, keepdims=False)
        lane_cols = jnp.transpose(group_lanes.reshape(ROWS_G, EXP_GRP).astype(jnp.float32))[:, :, None]
        first = (group_now * EXP_GRP).astype(jnp.int32)
        gate_w = lax.dynamic_slice_in_dim(w_gate, first, EXP_GRP, 0)
        up_w = lax.dynamic_slice_in_dim(w_up, first, EXP_GRP, 0)
        down_w = lax.dynamic_slice_in_dim(w_down, first, EXP_GRP, 0)
        gate_saved = lax.dynamic_slice_in_dim(saved_gate, first, EXP_GRP, 0)
        up_saved = lax.dynamic_slice_in_dim(saved_up, first, EXP_GRP, 0)
        group_grad = jnp.zeros((ROWS_G, D), jnp.float32)
        for hidden_part in range(N_LOCAL):
            low_edge = hidden_part * hidden_blk
            high_edge = low_edge + hidden_blk
            hidden_grad = jnp.einsum("rd,ehd->erh", dispatched, down_w[:, low_edge:high_edge, :].astype(jnp.float32))
            grad_gate, grad_up = expert_grads(hidden_grad, lane_cols, gate_saved[:, :, low_edge:high_edge], up_saved[:, :, low_edge:high_edge])
            piece_sum = jnp.einsum("erh,edh->rd", grad_gate.astype(jnp.float32), gate_w[:, :, low_edge:high_edge].astype(jnp.float32))
            piece_sum = piece_sum + jnp.einsum("erh,edh->rd", grad_up.astype(jnp.float32), up_w[:, :, low_edge:high_edge].astype(jnp.float32))
            rounded = lax.optimization_barrier(piece_sum.astype(jnp.bfloat16))
            group_grad = group_grad + rounded.astype(jnp.float32)
        running = running + jnp.einsum("sct,scd->std", group_tables, group_grad.reshape(N_GROUP, CAP, D), precision=lax.Precision.HIGHEST)
        return running, None

    start_value = jnp.zeros((N_GROUP, TOK_GRP, D), jnp.float32)
    running, unused = lax.scan(per_group, start_value, jnp.arange(N_GROUP, dtype=jnp.int32))
    return running.reshape(TOKENS, D).astype(jnp.bfloat16)
```

```python
import jax
import jax.numpy as jnp
from jax import lax
from jax.experimental import pallas as pl
from jax.experimental.pallas import tpu as pltpu
from jax.sharding import PartitionSpec as P

EXP_GRP = 3
CAP = 64
LANE_ROWS = 8
Z_LAST = (0, 32)
Z_FIRST = ((32, 16), (48, 16))
Z_OFFSETS = (0, -1, 1, 2)
VMEM = 40 * 1024 * 1024
BF = jnp.bfloat16
F32 = jnp.float32
NT = (((1,), (1,)), ((), ()))
TN = (((0,), (0,)), ((), ()))


def params(limit=VMEM):
    return pltpu.CompilerParams(vmem_limit_bytes=limit)


def cost(flops, nbytes):
    return pl.CostEstimate(flops=int(flops), bytes_accessed=int(nbytes), transcendentals=0)


def routing_kernel(groups_ref, picks_ref, weights_ref, tok_ref, table_ref, out_ref):
    group_count, slots, tok_rows = table_ref.shape
    first = out_ref.shape[1] - LANE_ROWS
    groups = groups_ref[...]
    picks = picks_ref[...]
    weights = weights_ref[...]
    ids = lax.broadcasted_iota(jnp.int32, (group_count, tok_rows), 0)
    member = jnp.zeros((group_count, tok_rows), jnp.bool_)
    for q in range(groups.shape[0]):
        member = member | (ids == groups[q : q + 1, :])
    earlier = lax.broadcasted_iota(jnp.int32, (tok_rows, tok_rows), 0) < lax.broadcasted_iota(
        jnp.int32, (tok_rows, tok_rows), 1
    )
    slot = jnp.dot(
        member.astype(F32).astype(BF), earlier.astype(F32).astype(BF), preferred_element_type=F32
    ).astype(jnp.int32)
    slot = jnp.where(member, slot, -1)
    slot_ids = lax.broadcasted_iota(jnp.int32, (group_count, slots, tok_rows), 1)
    table = (slot[:, None, :] == slot_ids).astype(F32).astype(BF)
    table_ref[...] = table

    shape = (group_count, LANE_ROWS, tok_rows)
    group_ids = lax.broadcasted_iota(jnp.int32, shape, 0)
    expert_ids = lax.broadcasted_iota(jnp.int32, shape, 1)
    spread = jnp.zeros(shape, F32)
    for k in range(picks.shape[0]):
        pick = picks[k : k + 1, :]
        chosen = jnp.zeros_like(pick)
        for q in range(groups.shape[0]):
            inside = (pick >= q * EXP_GRP) & (pick < (q + 1) * EXP_GRP)
            chosen = chosen + jnp.where(inside, groups[q : q + 1, :] * EXP_GRP + pick - q * EXP_GRP, 0)
        hit = group_ids * EXP_GRP + expert_ids == chosen[:, None, :]
        hit = hit & (expert_ids < EXP_GRP)
        spread = spread + jnp.where(hit, weights[k : k + 1, :][:, None, :], 0.0)
    spread = spread.astype(BF)

    width = out_ref.shape[2]
    rows = jnp.dot(
        table[:, :first].reshape(group_count * first, tok_rows), tok_ref[...], preferred_element_type=F32
    ).astype(BF)
    out_ref[:, :first, :] = rows.reshape(group_count, first, width)
    out_ref[:, first:, :] = jnp.zeros((group_count, LANE_ROWS, width), BF)
    for g in range(group_count):
        lanes = lax.dot_general(spread[g], table[g], NT, preferred_element_type=F32)
        out_ref[g, first:, :slots] = lanes.astype(BF)


def route(token_groups, expert_pick, combine_weight, tokens, group_count):
    tok_rows, width = tokens.shape
    first = Z_LAST[1]
    return pl.pallas_call(
        routing_kernel,
        out_shape=(
            jax.ShapeDtypeStruct((group_count, CAP, tok_rows), BF),
            jax.ShapeDtypeStruct((group_count, first + LANE_ROWS, width), BF),
        ),
        compiler_params=params(),
        cost_estimate=cost(2 * group_count * first * tok_rows * width, 4e6),
        name="route",
    )(token_groups.T, expert_pick.T, combine_weight.T, tokens)


def spread_kernel(table_ref, t0, t1, t2, t3, out_ref):
    group_count, slots, tok_rows = table_ref.shape
    table = table_ref[...].reshape(group_count * slots, tok_rows)
    for z, tok in enumerate((t0, t1, t2, t3)):
        rows = jnp.dot(table, tok[...], preferred_element_type=F32).astype(BF)
        out_ref[:, z] = rows.reshape(group_count, slots, rows.shape[1])


def spread_tokens(table, tokens):
    group_count, slots, tok_rows = table.shape
    width = tokens[0].shape[1]
    return pl.pallas_call(
        spread_kernel,
        out_shape=jax.ShapeDtypeStruct((group_count, len(tokens), slots, width), BF),
        compiler_params=params(),
        cost_estimate=cost(8 * group_count * slots * tok_rows * width, 8 * group_count * slots * width),
        name="spread",
    )(table, *tokens)


def write_grads(hidden, lane_ref, gate_ref, up_ref, out_ref):
    rows = hidden.shape[0]
    units = gate_ref.shape[-1]
    lanes = lane_ref[...].reshape(rows, EXP_GRP)
    for j in range(EXP_GRP):
        scaled = hidden[:, j * units : (j + 1) * units] * lanes[:, j : j + 1]
        p = gate_ref[j].reshape(rows, units).astype(F32)
        q = up_ref[j].reshape(rows, units).astype(F32)
        sg = 1.0 / (1.0 + jnp.exp(-p))
        gate = scaled * q * sg * (1.0 + p * (1.0 - sg))
        up = scaled * p * sg
        out_ref[:, j * units : (j + 1) * units] = gate.astype(BF)
        out_ref[:, (EXP_GRP + j) * units : (EXP_GRP + j + 1) * units] = up.astype(BF)


def hidden_last_kernel(order, x_ref, down_ref, lane_ref, gate_ref, up_ref, out_ref, total):
    step = pl.program_id(0)
    part = lax.dot_general(x_ref[0], down_ref[...], NT, preferred_element_type=F32)

    @pl.when(step == 0)
    def _():
        total[...] = part

    @pl.when(step > 0)
    def _():
        total[...] += part

    @pl.when(step == pl.num_programs(0) - 1)
    def _():
        write_grads(total[...], lane_ref, gate_ref, up_ref, out_ref)


def hidden_first_kernel(order, own_ref, other_ref, down_ref, lane_ref, gate_ref, up_ref, out_ref, total):
    step = pl.program_id(0)
    rows, width = out_ref.shape[0], own_ref.shape[-1]
    half = pl.num_programs(0) // 2

    @pl.when(step == 0)
    def _():
        total[...] = jnp.zeros_like(total)

    @pl.when(step < half)
    def _():
        total[...] += lax.dot_general(
            own_ref[...].reshape(rows, width), down_ref[...], NT, preferred_element_type=F32
        )

    @pl.when(step >= half)
    def _():
        total[...] += lax.dot_general(
            other_ref[...].reshape(rows, width), down_ref[...], NT, preferred_element_type=F32
        )

    @pl.when(step == pl.num_programs(0) - 1)
    def _():
        write_grads(total[...], lane_ref, gate_ref, up_ref, out_ref)


def hidden_grads(order, rows_in, w_down, lanes, saved_gate, saved_up, slots):
    start, count = slots
    units = w_down.shape[0]
    blocks = order.shape[0]
    width = w_down.shape[1] // blocks
    group_count = lanes.shape[0]
    rows = group_count * count
    if len(rows_in) == 1:
        kernel = hidden_last_kernel
        row_specs = [pl.BlockSpec((1, rows, width), lambda i, o: (i, 0, 0))]
    else:
        kernel = hidden_first_kernel
        half = blocks // 2
        row_specs = [
            pl.BlockSpec((group_count, 1, count, width), lambda i, o: (0, jnp.minimum(i, half - 1), 0, 0)),
            pl.BlockSpec((group_count, 1, count, width), lambda i, o: (0, jnp.maximum(i - half, 0), 0, 0)),
        ]
    saved_spec = pl.BlockSpec(
        (EXP_GRP, group_count, count, units // EXP_GRP), lambda i, o: (0, 0, start // count, 0)
    )
    return pl.pallas_call(
        kernel,
        out_shape=jax.ShapeDtypeStruct((rows, 2 * units), BF),
        grid_spec=pltpu.PrefetchScalarGridSpec(
            num_scalar_prefetch=1,
            grid=(blocks,),
            in_specs=row_specs
            + [
                pl.BlockSpec((units, width), lambda i, o: (0, o[i])),
                pl.BlockSpec((group_count, count, EXP_GRP), lambda i, o: (0, start // count, 0)),
                saved_spec,
                saved_spec,
            ],
            out_specs=pl.BlockSpec((rows, 2 * units), lambda i, o: (0, 0)),
            scratch_shapes=[pltpu.VMEM((rows, units), F32)],
        ),
        compiler_params=params(),
        cost_estimate=cost(
            2 * rows * units * blocks * width, 2 * (rows + units) * blocks * width + 8 * rows * units
        ),
        name="hidden",
    )(order, *rows_in, w_down, lanes, saved_gate, saved_up)


def weights_times(grads_ref, gate_ref, up_ref):
    columns = jnp.concatenate(
        [gate_ref[j] for j in range(EXP_GRP)] + [up_ref[j] for j in range(EXP_GRP)], axis=1
    )
    return lax.dot_general(grads_ref[...], columns, NT, preferred_element_type=F32)


def back_last_kernel(order, grads_ref, gate_ref, up_ref, out_ref):
    out_ref[0] = weights_times(grads_ref, gate_ref, up_ref).astype(BF)


def back_first_kernel(order, grads_ref, gate_ref, up_ref, out_ref):
    group_count, _, count, width = out_ref.shape
    part = weights_times(grads_ref, gate_ref, up_ref)
    out_ref[...] = part.astype(BF).reshape(group_count, 1, count, width)


def back_add_kernel(order, grads_ref, gate_ref, up_ref, other_ref, out_ref):
    group_count, _, count, width = out_ref.shape
    part = weights_times(grads_ref, gate_ref, up_ref)
    part = part + other_ref[...].reshape(group_count * count, width).astype(F32)
    out_ref[...] = part.astype(BF).reshape(group_count, 1, count, width)


def back(order, grads, w_gate, w_up, group_count, other=None, last=False):
    rows, depth = grads.shape
    blocks = order.shape[0]
    width = w_gate.shape[1] // (blocks if last else 2 * blocks)
    units = w_gate.shape[2]
    weight_spec = pl.BlockSpec((EXP_GRP, width, units), lambda i, o: (0, o[i], 0))
    in_specs = [pl.BlockSpec((rows, depth), lambda i, o: (0, 0)), weight_spec, weight_spec]
    operands = [order, grads, w_gate, w_up]
    if last:
        kernel = back_last_kernel
        out_shape = (blocks, rows, width)
        out_spec = pl.BlockSpec((1, rows, width), lambda i, o: (i, 0, 0))
    else:
        kernel = back_first_kernel
        count = rows // group_count
        out_shape = (group_count, blocks, count, width)
        out_spec = pl.BlockSpec((group_count, 1, count, width), lambda i, o: (0, i, 0, 0))
        if other is not None:
            kernel = back_add_kernel
            in_specs.append(out_spec)
            operands.append(other)
    return pl.pallas_call(
        kernel,
        out_shape=jax.ShapeDtypeStruct(out_shape, BF),
        grid_spec=pltpu.PrefetchScalarGridSpec(
            num_scalar_prefetch=1, grid=(blocks,), in_specs=in_specs, out_specs=out_spec
        ),
        compiler_params=params(),
        cost_estimate=cost(
            2 * rows * depth * blocks * width, 2 * (rows + depth) * blocks * width + 2 * rows * depth
        ),
        name="back",
    )(*operands)


def collect_kernel(*refs):
    count = len(Z_FIRST)
    tables, arrived, outs = refs[:count], refs[count : 2 * count], refs[2 * count :]
    group_count, slots, tok_rows = tables[0].shape
    width = arrived[0].shape[-1]
    for z, out in enumerate(outs):
        total = jnp.zeros((tok_rows, width), F32)
        for table, rows in zip(tables, arrived):
            total = total + lax.dot_general(
                table[...].reshape(group_count * slots, tok_rows),
                rows[:, z].reshape(group_count * slots, width),
                TN,
                preferred_element_type=F32,
            )
        out[...] = total.astype(out.dtype)


def collect(tables, arrived):
    group_count, slots, tok_rows = tables[0].shape
    width = arrived[0].shape[-1]
    return pl.pallas_call(
        collect_kernel,
        out_shape=tuple(
            jax.ShapeDtypeStruct((tok_rows, width), F32 if z == 0 else BF) for z in range(len(Z_OFFSETS))
        ),
        compiler_params=params(),
        cost_estimate=cost(16 * group_count * slots * tok_rows * width, 16 * group_count * slots * width),
        name="collect",
    )(*tables, *arrived)


def finish_kernel(table_ref, rows_ref, own_ref, a_ref, b_ref, c_ref, out_ref):
    group_count, slots, tok_rows = table_ref.shape
    width = rows_ref.shape[-1]
    total = lax.dot_general(
        table_ref[...].reshape(group_count * slots, tok_rows),
        rows_ref[...].reshape(group_count * slots, width),
        TN,
        preferred_element_type=F32,
    )
    total = total + own_ref[...]
    for ref in (a_ref, b_ref, c_ref):
        total = total + ref[...].astype(F32)
    out_ref[...] = total.astype(BF)


def finish(table, rows, own, others):
    tok_rows, width = own.shape
    return pl.pallas_call(
        finish_kernel,
        out_shape=jax.ShapeDtypeStruct((tok_rows, width), BF),
        compiler_params=params(),
        cost_estimate=cost(2 * table.shape[0] * table.shape[1] * tok_rows * width, 3e6),
        name="finish",
    )(table, rows, own, *others)


def on_device(
    grad_out, combine_weight, token_groups, expert_pick, saved_gate, saved_up, w_gate, w_up, w_down
):
    group_count = lax.axis_size("group")
    local_count = lax.axis_size("local")
    chips = local_count // 2
    place = lax.axis_index("local")
    z, core = place // 2, place % 2
    offsets = jnp.array(Z_OFFSETS, jnp.int32)
    own_order = ((z + offsets) % chips) * 2 + core
    other_order = ((z + offsets) % chips) * 2 + 1 - core
    all_order = jnp.arange(local_count, dtype=jnp.int32)

    def shift(value, by):
        pairs = [
            (c * 2 + k, ((c + by) % chips) * 2 + k) for c in range(chips) for k in range(2)
        ]
        return lax.ppermute(value, "local", pairs)

    def swap(value):
        return lax.ppermute(value, "local", [(i, i ^ 1) for i in range(local_count)])

    def exchange(value):
        return lax.all_to_all(value, "group", split_axis=0, concat_axis=0, tiled=True)

    units = w_gate.shape[2]
    down = w_down.reshape(EXP_GRP * units, w_down.shape[2])
    gate_slots = saved_gate.reshape(EXP_GRP, group_count, CAP, units)
    up_slots = saved_up.reshape(EXP_GRP, group_count, CAP, units)

    blocks = [grad_out] + [shift(grad_out, -by) for by in Z_OFFSETS[1:]]
    table, first_out = route(token_groups, expert_pick, combine_weight, grad_out, group_count)
    first_count = Z_LAST[1]
    first_in = exchange(first_out)
    lanes = jnp.transpose(first_in[:, first_count : first_count + EXP_GRP, :CAP], (0, 2, 1)).astype(F32)
    width = grad_out.shape[1]
    last_rows = lax.all_gather(
        first_in[:, :first_count].reshape(group_count * first_count, width), "local", axis=0, tiled=False
    )

    tables = [table[:, start : start + count] for start, count in Z_FIRST]
    own = [exchange(spread_tokens(t, blocks)) for t in tables]
    other = [swap(rows) for rows in own]

    last_grads = hidden_grads(all_order, [last_rows], down, lanes, gate_slots, up_slots, Z_LAST)
    last_part = back(all_order, last_grads, w_gate, w_up, group_count, last=True)
    last_sum = lax.psum_scatter(last_part, "local", scatter_dimension=0, tiled=False)

    returned = []
    for slots, mine, theirs in zip(Z_FIRST, own, other):
        grads = hidden_grads(
            jnp.concatenate([own_order, other_order]), [mine, theirs], down, lanes, gate_slots, up_slots, slots
        )
        away = swap(back(other_order, grads, w_gate, w_up, group_count))
        returned.append(exchange(back(own_order, grads, w_gate, w_up, group_count, other=away)))

    last_home = exchange(last_sum.reshape(group_count, first_count, width))
    pieces = collect(tables, returned)
    others = [shift(piece, by) for piece, by in zip(pieces[1:], Z_OFFSETS[1:])]
    return finish(table[:, :first_count], last_home, pieces[0], others)


def solution(mesh):
    placed = (
        P("group", "local"),
        P("group", None),
        P("group", None),
        P("group", None),
        P("group", None, "local"),
        P("group", None, "local"),
        P("group", None, "local"),
        P("group", None, "local"),
        P("group", "local", None),
    )
    return jax.shard_map(
        on_device, mesh=mesh, in_specs=placed, out_specs=P("group", "local"), check_vma=False
    )
```

```python
import functools

import jax
import jax.numpy as jnp
from jax import lax
from jax.experimental import pallas as pl
from jax.experimental.pallas import tpu as pltpu
from jax.sharding import PartitionSpec as P

EXP_GRP = 3
CAP = 64
LANE_ROWS = 8
Z_LAST = (0, 32)
Z_FIRST = ((32, 16), (48, 16))
Z_OFFSETS = (0, -1, 1, 2)
VMEM = 60 * 1024 * 1024
BF = jnp.bfloat16
F32 = jnp.float32
NT = (((1,), (1,)), ((), ()))
TN = (((0,), (0,)), ((), ()))


def params():
    return pltpu.CompilerParams(vmem_limit_bytes=VMEM)


COST = pl.CostEstimate(flops=1000, bytes_accessed=1000, transcendentals=0)


def after(value, *earlier):
    return lax.optimization_barrier((value, *earlier))[0]


def routing_kernel(groups_ref, picks_ref, weights_ref, tok_ref, table_ref, out_ref):
    group_count, slots, tok_rows = table_ref.shape
    first = out_ref.shape[1] - LANE_ROWS
    groups = groups_ref[...]
    picks = picks_ref[...]
    weights = weights_ref[...]
    ids = lax.broadcasted_iota(jnp.int32, (group_count, tok_rows), 0)
    member = jnp.zeros((group_count, tok_rows), jnp.bool_)
    for q in range(groups.shape[0]):
        member = member | (ids == groups[q : q + 1, :])
    earlier = lax.broadcasted_iota(jnp.int32, (tok_rows, tok_rows), 0) < lax.broadcasted_iota(
        jnp.int32, (tok_rows, tok_rows), 1
    )
    slot = jnp.dot(
        member.astype(F32).astype(BF), earlier.astype(F32).astype(BF), preferred_element_type=F32
    ).astype(jnp.int32)
    slot = jnp.where(member, slot, -1)
    slot_ids = lax.broadcasted_iota(jnp.int32, (group_count, slots, tok_rows), 1)
    table = (slot[:, None, :] == slot_ids).astype(F32).astype(BF)
    table_ref[...] = table

    shape = (group_count, LANE_ROWS, tok_rows)
    group_ids = lax.broadcasted_iota(jnp.int32, shape, 0)
    expert_ids = lax.broadcasted_iota(jnp.int32, shape, 1)
    spread = jnp.zeros(shape, F32)
    for k in range(picks.shape[0]):
        pick = picks[k : k + 1, :]
        chosen = jnp.zeros_like(pick)
        for q in range(groups.shape[0]):
            inside = (pick >= q * EXP_GRP) & (pick < (q + 1) * EXP_GRP)
            chosen = chosen + jnp.where(inside, groups[q : q + 1, :] * EXP_GRP + pick - q * EXP_GRP, 0)
        hit = group_ids * EXP_GRP + expert_ids == chosen[:, None, :]
        hit = hit & (expert_ids < EXP_GRP)
        spread = spread + jnp.where(hit, weights[k : k + 1, :][:, None, :], 0.0)
    spread = spread.astype(BF)

    width = out_ref.shape[2]
    rows = jnp.dot(
        table[:, :first].reshape(group_count * first, tok_rows), tok_ref[...], preferred_element_type=F32
    ).astype(BF)
    out_ref[:, :first, :] = rows.reshape(group_count, first, width)
    out_ref[:, first:, :] = jnp.zeros((group_count, LANE_ROWS, width), BF)
    for g in range(group_count):
        lanes = lax.dot_general(spread[g], table[g], NT, preferred_element_type=F32)
        out_ref[g, first:, :slots] = lanes.astype(BF)


def route(token_groups, expert_pick, combine_weight, tokens, group_count):
    tok_rows, width = tokens.shape
    first = Z_LAST[1]
    return pl.pallas_call(
        routing_kernel,
        out_shape=(
            jax.ShapeDtypeStruct((group_count, CAP, tok_rows), BF),
            jax.ShapeDtypeStruct((group_count, first + LANE_ROWS, width), BF),
        ),
        compiler_params=params(),
        cost_estimate=COST,
        name="route",
    )(token_groups.T, expert_pick.T, combine_weight.T, tokens)


def spread_kernel(table_ref, t0, t1, t2, t3, out_ref):
    group_count, slots, tok_rows = table_ref.shape
    table = table_ref[...].reshape(group_count * slots, tok_rows)
    for z, tok in enumerate((t0, t1, t2, t3)):
        rows = jnp.dot(table, tok[...], preferred_element_type=F32).astype(BF)
        out_ref[:, z] = rows.reshape(group_count, slots, rows.shape[1])


def spread_tokens(table, tokens):
    group_count, slots, tok_rows = table.shape
    width = tokens[0].shape[1]
    return pl.pallas_call(
        spread_kernel,
        out_shape=jax.ShapeDtypeStruct((group_count, len(tokens), slots, width), BF),
        compiler_params=params(),
        cost_estimate=COST,
        name="spread",
    )(table, *tokens)


def write_grads(hidden, lane_ref, gate_ref, up_ref, out_ref):
    rows = hidden.shape[0]
    units = gate_ref.shape[-1]
    lanes = lane_ref[...].reshape(rows, EXP_GRP)
    for j in range(EXP_GRP):
        scaled = hidden[:, j * units : (j + 1) * units] * lanes[:, j : j + 1]
        p = gate_ref[j].reshape(rows, units).astype(F32)
        q = up_ref[j].reshape(rows, units).astype(F32)
        sg = 1.0 / (1.0 + jnp.exp(-p))
        gate = scaled * q * sg * (1.0 + p * (1.0 - sg))
        up = scaled * p * sg
        out_ref[:, j * units : (j + 1) * units] = gate.astype(BF)
        out_ref[:, (EXP_GRP + j) * units : (EXP_GRP + j + 1) * units] = up.astype(BF)


ANY = pl.BlockSpec(memory_space=pl.ANY)


def block_orders(chips):
    place = lax.axis_index("local")
    z, core = lax.div(place, 2), lax.rem(place, 2)
    starts = [lax.rem(z + by + chips, chips) * 2 for by in Z_OFFSETS]
    return [start + core for start in starts], [start + 1 - core for start in starts]


def columns_of(ref, block, width):
    return ref.at[:, pl.ds(pl.multiple_of(block * width, 128), width)]


def rows_of(ref, block, width):
    return ref.at[:, pl.ds(pl.multiple_of(block * width, 128), width)]


def copies_of(pairs, sems):
    return [pltpu.make_async_copy(src, dst, sems.at[i]) for i, (src, dst) in enumerate(pairs)]


def begin(copies):
    for copy in copies:
        copy.start()
    return copies


class Stream:
    def __init__(self, groups, depth=3):
        self.groups, self.depth, self.next = groups, depth, 0
        self.ahead(depth)

    def ahead(self, until):
        while self.next < min(until, len(self.groups)):
            begin(self.groups[self.next])
            self.next += 1

    def use(self, index):
        self.ahead(index + 1 + self.depth)
        for copy in self.groups[index]:
            copy.wait()


def saved_copies(start, count, lane_ref, gate_ref, up_ref, lane, gate, up, sems):
    slots = pl.ds(start, count)
    return copies_of(
        [(lane_ref.at[:, slots], lane), (gate_ref.at[:, :, slots], gate), (up_ref.at[:, :, slots], up)], sems
    )


def weights_times(grads, gate, up):
    columns = jnp.concatenate([gate[j] for j in range(EXP_GRP)] + [up[j] for j in range(EXP_GRP)], axis=1)
    return lax.dot_general(grads, columns, NT, preferred_element_type=F32)


def last_kernel(
    x_ref, down_ref, w_gate_ref, w_up_ref, lane_ref, gate_ref, up_ref, out_ref,
    x, down, w_gate, w_up, lane, gate, up, grads, out,
    x_sems, down_sems, w_gate_sems, w_up_sems, saved_sems, out_sems,
):
    blocks, _, width = x_ref.shape
    start, count = Z_LAST
    turns = out.shape[0]
    groups = [
        copies_of([(x_ref.at[k], x.at[k])], x_sems.at[pl.ds(k, 1)])
        + copies_of([(columns_of(down_ref, k, width), down.at[k])], down_sems.at[pl.ds(k, 1)])
        for k in range(blocks)
    ]
    groups[-1] += saved_copies(start, count, lane_ref, gate_ref, up_ref, lane, gate, up, saved_sems)
    groups += [
        copies_of([(rows_of(w_gate_ref, k, width), w_gate.at[k])], w_gate_sems.at[pl.ds(k, 1)])
        + copies_of([(rows_of(w_up_ref, k, width), w_up.at[k])], w_up_sems.at[pl.ds(k, 1)])
        for k in range(blocks)
    ]
    stream = Stream(groups)
    total = None
    for k in range(blocks):
        stream.use(k)
        part = lax.dot_general(x[k], down[k], NT, preferred_element_type=F32)
        total = part if total is None else total + part
    write_grads(total, lane, gate, up, grads)
    leaving = []
    for k in range(blocks):
        stream.use(blocks + k)
        if k >= turns:
            leaving[k - turns].wait()
        out[k % turns] = weights_times(grads[...], w_gate[k], w_up[k]).astype(BF)
        leaving += begin(copies_of([(out.at[k % turns], out_ref.at[k])], out_sems.at[pl.ds(k, 1)]))
    for copy in leaving[-turns:]:
        copy.wait()


def last_pass(rows_in, w_down, w_gate, w_up, lanes, saved_gate, saved_up):
    blocks, rows, width = rows_in.shape
    units = w_gate.shape[2]
    group_count = lanes.shape[0]
    count = Z_LAST[1]
    sems = pltpu.SemaphoreType.DMA
    return pl.pallas_call(
        last_kernel,
        out_shape=jax.ShapeDtypeStruct((blocks, rows, width), BF),
        in_specs=[ANY] * 7,
        out_specs=ANY,
        scratch_shapes=[
            pltpu.VMEM((blocks, rows, width), BF),
            pltpu.VMEM((blocks, EXP_GRP * units, width), BF),
            pltpu.VMEM((blocks, EXP_GRP, width, units), BF),
            pltpu.VMEM((blocks, EXP_GRP, width, units), BF),
            pltpu.VMEM((group_count, count, EXP_GRP), F32),
            pltpu.VMEM((EXP_GRP, group_count, count, units), BF),
            pltpu.VMEM((EXP_GRP, group_count, count, units), BF),
            pltpu.VMEM((rows, 2 * EXP_GRP * units), BF),
            pltpu.VMEM((3, rows, width), BF),
            sems((blocks,)), sems((blocks,)), sems((blocks,)), sems((blocks,)), sems((3,)), sems((blocks,)),
        ],
        compiler_params=params(),
        cost_estimate=COST,
        name="last_pass",
    )(rows_in, w_down, w_gate, w_up, lanes, saved_gate, saved_up)


def first_kernel(
    start, own_ref, other_ref, down_ref, w_gate_ref, w_up_ref, lane_ref, gate_ref, up_ref, *refs
):
    chips, width = own_ref.shape[1], own_ref.shape[3]
    grads_ref, out_refs, refs = refs[0], refs[1 : 1 + chips], refs[1 + chips :]
    own, other, down, w_gate, w_up, lane, gate, up, grads, out = refs[:10]
    own_sems, other_sems, down_sems, w_gate_sems, w_up_sems, saved_sems, out_sems, grads_sems = refs[10:]
    mine, theirs = block_orders(chips)
    order = mine + theirs
    count = own_ref.shape[2]
    rows = own_ref.shape[0] * count
    groups = []
    for k in range(2 * chips):
        src, dst, sems = (own_ref, own, own_sems) if k < chips else (other_ref, other, other_sems)
        groups.append(
            copies_of([(src.at[:, k % chips], dst.at[k % chips])], sems.at[pl.ds(k % chips, 1)])
            + copies_of([(columns_of(down_ref, order[k], width), down.at[k])], down_sems.at[pl.ds(k, 1)])
        )
    groups[-1] += saved_copies(start, count, lane_ref, gate_ref, up_ref, lane, gate, up, saved_sems)
    for k in range(chips):
        block = order[chips + k]
        groups.append(
            copies_of([(rows_of(w_gate_ref, block, width), w_gate.at[k])], w_gate_sems.at[pl.ds(k, 1)])
            + copies_of([(rows_of(w_up_ref, block, width), w_up.at[k])], w_up_sems.at[pl.ds(k, 1)])
        )
    stream = Stream(groups)
    total = None
    for k in range(2 * chips):
        stream.use(k)
        piece = own[k] if k < chips else other[k - chips]
        part = lax.dot_general(piece.reshape(rows, width), down[k], NT, preferred_element_type=F32)
        total = part if total is None else total + part
    write_grads(total, lane, gate, up, grads)
    leaving = begin(copies_of([(grads, grads_ref)], grads_sems))
    for k in range(chips):
        stream.use(2 * chips + k)
        out[k] = weights_times(grads[...], w_gate[k], w_up[k]).astype(BF)
        leaving += begin(copies_of([(out.at[k], out_refs[k])], out_sems.at[pl.ds(k, 1)]))
    for copy in leaving:
        copy.wait()


def first_pass(own, other, w_down, w_gate, w_up, lanes, saved_gate, saved_up, slots):
    start, count = slots
    group_count, chips, _, width = own.shape
    units = w_gate.shape[2]
    rows = group_count * count
    sems = pltpu.SemaphoreType.DMA
    results = pl.pallas_call(
        functools.partial(first_kernel, start),
        out_shape=(jax.ShapeDtypeStruct((rows, 2 * EXP_GRP * units), BF),)
        + tuple(jax.ShapeDtypeStruct((rows, width), BF) for _ in range(chips)),
        in_specs=[ANY] * 8,
        out_specs=(ANY,) * (1 + chips),
        scratch_shapes=[
            pltpu.VMEM((chips, group_count, count, width), BF),
            pltpu.VMEM((chips, group_count, count, width), BF),
            pltpu.VMEM((2 * chips, EXP_GRP * units, width), BF),
            pltpu.VMEM((chips, EXP_GRP, width, units), BF),
            pltpu.VMEM((chips, EXP_GRP, width, units), BF),
            pltpu.VMEM((group_count, count, EXP_GRP), F32),
            pltpu.VMEM((EXP_GRP, group_count, count, units), BF),
            pltpu.VMEM((EXP_GRP, group_count, count, units), BF),
            pltpu.VMEM((rows, 2 * EXP_GRP * units), BF),
            pltpu.VMEM((chips, rows, width), BF),
            sems((chips,)), sems((chips,)), sems((2 * chips,)), sems((chips,)), sems((chips,)), sems((3,)),
            sems((chips,)), sems((1,)),
        ],
        compiler_params=params(),
        cost_estimate=COST,
        name="first_pass",
    )(own, other, w_down, w_gate, w_up, lanes, saved_gate, saved_up)
    return results[0], list(results[1:])


def own_kernel(grads_ref, w_gate_ref, w_up_ref, *refs):
    chips = len(refs) - 11
    other_refs, out_ref, refs = refs[:chips], refs[chips], refs[chips + 1 :]
    w_gate, w_up, other, grads, out, w_gate_sems, w_up_sems, other_sems, grads_sems, out_sems = refs
    group_count, _, count, width = out_ref.shape
    order = block_orders(chips)[0]
    arriving = begin(copies_of([(grads_ref, grads)], grads_sems))
    stream = Stream(
        [
            copies_of([(rows_of(w_gate_ref, order[k], width), w_gate.at[k])], w_gate_sems.at[pl.ds(k, 1)])
            + copies_of([(rows_of(w_up_ref, order[k], width), w_up.at[k])], w_up_sems.at[pl.ds(k, 1)])
            + copies_of([(other_refs[k], other.at[k])], other_sems.at[pl.ds(k, 1)])
            for k in range(chips)
        ],
        depth=2,
    )
    leaving = []
    for k in range(chips):
        stream.use(k)
        if k == 0:
            arriving[0].wait()
        part = weights_times(grads[...], w_gate[k], w_up[k]) + other[k].astype(F32)
        out[k] = part.astype(BF).reshape(group_count, count, width)
        leaving += begin(copies_of([(out.at[k], out_ref.at[:, k])], out_sems.at[pl.ds(k, 1)]))
    for copy in leaving:
        copy.wait()


def own_pass(grads, w_gate, w_up, others, group_count):
    rows, width = others[0].shape
    chips = len(others)
    count = rows // group_count
    units = w_gate.shape[2]
    sems = pltpu.SemaphoreType.DMA
    return pl.pallas_call(
        own_kernel,
        out_shape=jax.ShapeDtypeStruct((group_count, chips, count, width), BF),
        in_specs=[ANY] * (3 + chips),
        out_specs=ANY,
        scratch_shapes=[
            pltpu.VMEM((chips, EXP_GRP, width, units), BF),
            pltpu.VMEM((chips, EXP_GRP, width, units), BF),
            pltpu.VMEM((chips, rows, width), BF),
            pltpu.VMEM((rows, grads.shape[1]), BF),
            pltpu.VMEM((chips, group_count, count, width), BF),
            sems((chips,)), sems((chips,)), sems((chips,)), sems((1,)), sems((chips,)),
        ],
        compiler_params=params(),
        cost_estimate=COST,
        name="own_pass",
    )(grads, w_gate, w_up, *others)


def collect_kernel(*refs):
    count = len(Z_FIRST)
    tables, arrived, outs = refs[:count], refs[count : 2 * count], refs[2 * count :]
    group_count, slots, tok_rows = tables[0].shape
    width = arrived[0].shape[-1]
    for z, out in enumerate(outs):
        total = jnp.zeros((tok_rows, width), F32)
        for table, rows in zip(tables, arrived):
            total = total + lax.dot_general(
                table[...].reshape(group_count * slots, tok_rows),
                rows[:, z].reshape(group_count * slots, width),
                TN,
                preferred_element_type=F32,
            )
        out[...] = total.astype(out.dtype)


def collect(tables, arrived):
    group_count, slots, tok_rows = tables[0].shape
    width = arrived[0].shape[-1]
    return pl.pallas_call(
        collect_kernel,
        out_shape=tuple(
            jax.ShapeDtypeStruct((tok_rows, width), F32 if z == 0 else BF) for z in range(len(Z_OFFSETS))
        ),
        compiler_params=params(),
        cost_estimate=COST,
        name="collect",
    )(*tables, *arrived)


def finish_kernel(table_ref, rows_ref, own_ref, a_ref, b_ref, c_ref, out_ref):
    group_count, slots, tok_rows = table_ref.shape
    width = rows_ref.shape[-1]
    total = lax.dot_general(
        table_ref[...].reshape(group_count * slots, tok_rows),
        rows_ref[...].reshape(group_count * slots, width),
        TN,
        preferred_element_type=F32,
    )
    total = total + own_ref[...]
    for ref in (a_ref, b_ref, c_ref):
        total = total + ref[...].astype(F32)
    out_ref[...] = total.astype(BF)


def finish(table, rows, own, others):
    tok_rows, width = own.shape
    return pl.pallas_call(
        finish_kernel,
        out_shape=jax.ShapeDtypeStruct((tok_rows, width), BF),
        compiler_params=params(),
        cost_estimate=COST,
        name="finish",
    )(table, rows, own, *others)


def on_device(
    grad_out, combine_weight, token_groups, expert_pick, saved_gate, saved_up, w_gate, w_up, w_down
):
    group_count = lax.axis_size("group")
    local_count = lax.axis_size("local")
    chips = local_count // 2
    def shift(value, by):
        pairs = [
            (c * 2 + k, ((c + by) % chips) * 2 + k) for c in range(chips) for k in range(2)
        ]
        return lax.ppermute(value, "local", pairs)

    def swap(value):
        return lax.ppermute(value, "local", [(i, i ^ 1) for i in range(local_count)])

    def exchange(value):
        return lax.all_to_all(value, "group", split_axis=0, concat_axis=0, tiled=True)

    units = w_gate.shape[2]
    down = w_down.reshape(EXP_GRP * units, w_down.shape[2])
    gate_slots = saved_gate.reshape(EXP_GRP, group_count, CAP, units)
    up_slots = saved_up.reshape(EXP_GRP, group_count, CAP, units)

    blocks = [grad_out] + [shift(grad_out, -by) for by in Z_OFFSETS[1:]]
    table, first_out = route(token_groups, expert_pick, combine_weight, grad_out, group_count)
    first_count = Z_LAST[1]
    first_in = exchange(first_out)
    lanes = jnp.transpose(first_in[:, first_count : first_count + EXP_GRP, :CAP], (0, 2, 1)).astype(F32)
    width = grad_out.shape[1]
    tables = [table[:, start : start + count] for start, count in Z_FIRST]
    sent = [spread_tokens(t, blocks) for t in tables]
    last_rows = lax.all_gather(
        after(first_in[:, :first_count].reshape(group_count * first_count, width), sent[0]),
        "local",
        axis=0,
        tiled=False,
    )

    own = [exchange(after(sent[0], lanes))]
    own[0], sent[1] = lax.optimization_barrier((own[0], sent[1]))
    other = [swap(own[0])]
    own.append(exchange(sent[1]))

    def first(k):
        grads, away = first_pass(own[k], other[k], down, w_gate, w_up, lanes, gate_slots, up_slots, Z_FIRST[k])
        return grads, [swap(piece) for piece in away]

    grads, others = first(0)
    last_part = last_pass(after(last_rows, grads), down, w_gate, w_up, lanes, gate_slots, up_slots)
    last_part, own[1], grads, *others = lax.optimization_barrier((last_part, own[1], grads, *others))
    last_sum = lax.psum_scatter(last_part, "local", scatter_dimension=0, tiled=False)
    ready = own_pass(grads, w_gate, w_up, others, group_count)
    first_home = exchange(ready)

    other.append(swap(own[1]))
    grads, others = first(1)
    second_home = exchange(after(own_pass(grads, w_gate, w_up, others, group_count), first_home))
    returned = [first_home, second_home]

    last_home = exchange(after(last_sum, second_home).reshape(group_count, first_count, width))
    pieces = collect(tables, returned)
    others = [shift(piece, by) for piece, by in zip(pieces[1:], Z_OFFSETS[1:])]
    return finish(table[:, :first_count], last_home, pieces[0], others)


def solution(mesh):
    placed = (
        P("group", "local"),
        P("group", None),
        P("group", None),
        P("group", None),
        P("group", None, "local"),
        P("group", None, "local"),
        P("group", None, "local"),
        P("group", None, "local"),
        P("group", "local", None),
    )
    return jax.shard_map(
        on_device, mesh=mesh, in_specs=placed, out_specs=P("group", "local"), check_vma=False
    )
```

```python
import functools

import jax
import jax.numpy as jnp
from jax import lax
from jax.experimental import pallas as pl
from jax.experimental.pallas import tpu as pltpu
from jax.sharding import PartitionSpec as P

EXP_GRP = 3
CAP = 64
LANE_ROWS = 8
Z_LAST = (0, 32)
Z_FIRST = ((32, 16), (48, 16))
Z_OFFSETS = (0, -1, 1, 2)
VMEM = 60 * 1024 * 1024
BF = jnp.bfloat16
F32 = jnp.float32
NT = (((1,), (1,)), ((), ()))
TN = (((0,), (0,)), ((), ()))


def params(limit=VMEM):
    return pltpu.CompilerParams(vmem_limit_bytes=limit)


COST = pl.CostEstimate(flops=1000, bytes_accessed=1000, transcendentals=0)


def after(value, *earlier):
    return lax.optimization_barrier((value, *earlier))[0]


def routing_kernel(groups_ref, picks_ref, weights_ref, tok_ref, table_ref, out_ref):
    group_count, slots, tok_rows = table_ref.shape
    first = out_ref.shape[1] - LANE_ROWS
    groups = groups_ref[...]
    picks = picks_ref[...]
    weights = weights_ref[...]
    ids = lax.broadcasted_iota(jnp.int32, (group_count, tok_rows), 0)
    member = jnp.zeros((group_count, tok_rows), jnp.bool_)
    for q in range(groups.shape[0]):
        member = member | (ids == groups[q : q + 1, :])
    earlier = lax.broadcasted_iota(jnp.int32, (tok_rows, tok_rows), 0) < lax.broadcasted_iota(
        jnp.int32, (tok_rows, tok_rows), 1
    )
    slot = jnp.dot(
        member.astype(F32).astype(BF), earlier.astype(F32).astype(BF), preferred_element_type=F32
    ).astype(jnp.int32)
    slot = jnp.where(member, slot, -1)
    slot_ids = lax.broadcasted_iota(jnp.int32, (group_count, slots, tok_rows), 1)
    table = (slot[:, None, :] == slot_ids).astype(F32).astype(BF)
    table_ref[...] = table

    shape = (group_count, LANE_ROWS, tok_rows)
    group_ids = lax.broadcasted_iota(jnp.int32, shape, 0)
    expert_ids = lax.broadcasted_iota(jnp.int32, shape, 1)
    spread = jnp.zeros(shape, F32)
    for k in range(picks.shape[0]):
        pick = picks[k : k + 1, :]
        chosen = jnp.zeros_like(pick)
        for q in range(groups.shape[0]):
            inside = (pick >= q * EXP_GRP) & (pick < (q + 1) * EXP_GRP)
            chosen = chosen + jnp.where(inside, groups[q : q + 1, :] * EXP_GRP + pick - q * EXP_GRP, 0)
        hit = group_ids * EXP_GRP + expert_ids == chosen[:, None, :]
        hit = hit & (expert_ids < EXP_GRP)
        spread = spread + jnp.where(hit, weights[k : k + 1, :][:, None, :], 0.0)
    spread = spread.astype(BF)

    width = out_ref.shape[2]
    rows = jnp.dot(
        table[:, :first].reshape(group_count * first, tok_rows), tok_ref[...], preferred_element_type=F32
    ).astype(BF)
    out_ref[:, :first, :] = rows.reshape(group_count, first, width)
    out_ref[:, first:, :] = jnp.zeros((group_count, LANE_ROWS, width), BF)
    for g in range(group_count):
        lanes = lax.dot_general(spread[g], table[g], NT, preferred_element_type=F32)
        out_ref[g, first:, :slots] = lanes.astype(BF)


def route(token_groups, expert_pick, combine_weight, tokens, group_count):
    tok_rows, width = tokens.shape
    first = Z_LAST[1]
    return pl.pallas_call(
        routing_kernel,
        out_shape=(
            jax.ShapeDtypeStruct((group_count, CAP, tok_rows), BF),
            jax.ShapeDtypeStruct((group_count, first + LANE_ROWS, width), BF),
        ),
        compiler_params=params(),
        cost_estimate=COST,
        name="route",
    )(token_groups.T, expert_pick.T, combine_weight.T, tokens)


def spread_kernel(table_ref, t0, t1, t2, t3, out_ref):
    group_count, slots, tok_rows = table_ref.shape
    table = table_ref[...].reshape(group_count * slots, tok_rows)
    for z, tok in enumerate((t0, t1, t2, t3)):
        rows = jnp.dot(table, tok[...], preferred_element_type=F32).astype(BF)
        out_ref[:, z] = rows.reshape(group_count, slots, rows.shape[1])


def spread_tokens(table, tokens):
    group_count, slots, tok_rows = table.shape
    width = tokens[0].shape[1]
    return pl.pallas_call(
        spread_kernel,
        out_shape=jax.ShapeDtypeStruct((group_count, len(tokens), slots, width), BF),
        compiler_params=params(),
        cost_estimate=COST,
        name="spread",
    )(table, *tokens)


def write_grads(hidden, lane_ref, gate_ref, up_ref, out_ref):
    rows = hidden.shape[0]
    units = gate_ref.shape[-1]
    lanes = lane_ref[...].reshape(rows, EXP_GRP)
    for j in range(EXP_GRP):
        scaled = hidden[:, j * units : (j + 1) * units] * lanes[:, j : j + 1]
        p = gate_ref[j].reshape(rows, units).astype(F32)
        q = up_ref[j].reshape(rows, units).astype(F32)
        sg = 1.0 / (1.0 + jnp.exp(-p))
        gate = scaled * q * sg * (1.0 + p * (1.0 - sg))
        up = scaled * p * sg
        out_ref[:, j * units : (j + 1) * units] = gate.astype(BF)
        out_ref[:, (EXP_GRP + j) * units : (EXP_GRP + j + 1) * units] = up.astype(BF)


ANY = pl.BlockSpec(memory_space=pl.ANY)


def block_orders(chips):
    place = lax.axis_index("local")
    z, core = lax.div(place, 2), lax.rem(place, 2)
    starts = [lax.rem(z + by + chips, chips) * 2 for by in Z_OFFSETS]
    return [start + core for start in starts], [start + 1 - core for start in starts]


def columns_of(ref, block, width):
    return ref.at[:, pl.ds(pl.multiple_of(block * width, 128), width)]


def rows_of(ref, block, width):
    return ref.at[:, pl.ds(pl.multiple_of(block * width, 128), width)]


def copies_of(pairs, sems):
    return [pltpu.make_async_copy(src, dst, sems.at[i]) for i, (src, dst) in enumerate(pairs)]


def begin(copies):
    for copy in copies:
        copy.start()
    return copies


class Stream:
    def __init__(self, groups, depth=3):
        self.groups, self.depth, self.next = groups, depth, 0
        self.ahead(depth)

    def ahead(self, until):
        while self.next < min(until, len(self.groups)):
            begin(self.groups[self.next])
            self.next += 1

    def use(self, index):
        self.ahead(index + 1 + self.depth)
        for copy in self.groups[index]:
            copy.wait()


def saved_copies(start, count, lane_ref, gate_ref, up_ref, lane, gate, up, sems):
    slots = pl.ds(start, count)
    return copies_of(
        [(lane_ref.at[:, slots], lane), (gate_ref.at[:, :, slots], gate), (up_ref.at[:, :, slots], up)], sems
    )


def weights_times(grads, gate, up):
    columns = jnp.concatenate([gate[j] for j in range(EXP_GRP)] + [up[j] for j in range(EXP_GRP)], axis=1)
    return lax.dot_general(grads, columns, NT, preferred_element_type=F32)


def last_kernel(
    x_ref, down_ref, w_gate_ref, w_up_ref, lane_ref, gate_ref, up_ref, out_ref,
    x, down, w_gate, w_up, lane, gate, up, grads, out,
    x_sems, down_sems, w_gate_sems, w_up_sems, saved_sems, out_sems,
):
    blocks, _, width = x_ref.shape
    start, count = Z_LAST
    turns = out.shape[0]
    groups = [
        copies_of([(x_ref.at[k], x.at[k])], x_sems.at[pl.ds(k, 1)])
        + copies_of([(columns_of(down_ref, k, width), down.at[k])], down_sems.at[pl.ds(k, 1)])
        for k in range(blocks)
    ]
    groups[-1] += saved_copies(start, count, lane_ref, gate_ref, up_ref, lane, gate, up, saved_sems)
    groups += [
        copies_of([(rows_of(w_gate_ref, k, width), w_gate.at[k])], w_gate_sems.at[pl.ds(k, 1)])
        + copies_of([(rows_of(w_up_ref, k, width), w_up.at[k])], w_up_sems.at[pl.ds(k, 1)])
        for k in range(blocks)
    ]
    stream = Stream(groups)
    total = None
    for k in range(blocks):
        stream.use(k)
        part = lax.dot_general(x[k], down[k], NT, preferred_element_type=F32)
        total = part if total is None else total + part
    write_grads(total, lane, gate, up, grads)
    leaving = []
    for k in range(blocks):
        stream.use(blocks + k)
        if k >= turns:
            leaving[k - turns].wait()
        out[k % turns] = weights_times(grads[...], w_gate[k], w_up[k]).astype(BF)
        leaving += begin(copies_of([(out.at[k % turns], out_ref.at[k])], out_sems.at[pl.ds(k, 1)]))
    for copy in leaving[-turns:]:
        copy.wait()


def last_pass(rows_in, w_down, w_gate, w_up, lanes, saved_gate, saved_up):
    blocks, rows, width = rows_in.shape
    units = w_gate.shape[2]
    group_count = lanes.shape[0]
    count = Z_LAST[1]
    sems = pltpu.SemaphoreType.DMA
    return pl.pallas_call(
        last_kernel,
        out_shape=jax.ShapeDtypeStruct((blocks, rows, width), BF),
        in_specs=[ANY] * 7,
        out_specs=ANY,
        scratch_shapes=[
            pltpu.VMEM((blocks, rows, width), BF),
            pltpu.VMEM((blocks, EXP_GRP * units, width), BF),
            pltpu.VMEM((blocks, EXP_GRP, width, units), BF),
            pltpu.VMEM((blocks, EXP_GRP, width, units), BF),
            pltpu.VMEM((group_count, count, EXP_GRP), F32),
            pltpu.VMEM((EXP_GRP, group_count, count, units), BF),
            pltpu.VMEM((EXP_GRP, group_count, count, units), BF),
            pltpu.VMEM((rows, 2 * EXP_GRP * units), BF),
            pltpu.VMEM((3, rows, width), BF),
            sems((blocks,)), sems((blocks,)), sems((blocks,)), sems((blocks,)), sems((3,)), sems((blocks,)),
        ],
        compiler_params=params(),
        cost_estimate=COST,
        name="last_pass",
    )(rows_in, w_down, w_gate, w_up, lanes, saved_gate, saved_up)


def first_kernel(
    start, own_ref, other_ref, down_ref, w_gate_ref, w_up_ref, lane_ref, gate_ref, up_ref, *refs
):
    chips, width = own_ref.shape[1], own_ref.shape[3]
    grads_ref, out_refs, refs = refs[0], refs[1 : 1 + chips], refs[1 + chips :]
    own, other, down, w_gate, w_up, lane, gate, up, grads, out = refs[:10]
    own_sems, other_sems, down_sems, w_gate_sems, w_up_sems, saved_sems, out_sems, grads_sems = refs[10:]
    mine, theirs = block_orders(chips)
    order = mine + theirs
    count = own_ref.shape[2]
    rows = own_ref.shape[0] * count
    groups = []
    for k in range(2 * chips):
        src, dst, sems = (own_ref, own, own_sems) if k < chips else (other_ref, other, other_sems)
        groups.append(
            copies_of([(src.at[:, k % chips], dst.at[k % chips])], sems.at[pl.ds(k % chips, 1)])
            + copies_of([(columns_of(down_ref, order[k], width), down.at[k])], down_sems.at[pl.ds(k, 1)])
        )
    groups[-1] += saved_copies(start, count, lane_ref, gate_ref, up_ref, lane, gate, up, saved_sems)
    for k in range(chips):
        block = order[chips + k]
        groups.append(
            copies_of([(rows_of(w_gate_ref, block, width), w_gate.at[k])], w_gate_sems.at[pl.ds(k, 1)])
            + copies_of([(rows_of(w_up_ref, block, width), w_up.at[k])], w_up_sems.at[pl.ds(k, 1)])
        )
    stream = Stream(groups)
    total = None
    for k in range(2 * chips):
        stream.use(k)
        piece = own[k] if k < chips else other[k - chips]
        part = lax.dot_general(piece.reshape(rows, width), down[k], NT, preferred_element_type=F32)
        total = part if total is None else total + part
    write_grads(total, lane, gate, up, grads)
    leaving = begin(copies_of([(grads, grads_ref)], grads_sems))
    for k in range(chips):
        stream.use(2 * chips + k)
        out[k] = weights_times(grads[...], w_gate[k], w_up[k]).astype(BF)
        leaving += begin(copies_of([(out.at[k], out_refs[k])], out_sems.at[pl.ds(k, 1)]))
    for copy in leaving:
        copy.wait()


def first_pass(own, other, w_down, w_gate, w_up, lanes, saved_gate, saved_up, slots):
    start, count = slots
    group_count, chips, _, width = own.shape
    units = w_gate.shape[2]
    rows = group_count * count
    sems = pltpu.SemaphoreType.DMA
    results = pl.pallas_call(
        functools.partial(first_kernel, start),
        out_shape=(jax.ShapeDtypeStruct((rows, 2 * EXP_GRP * units), BF),)
        + tuple(jax.ShapeDtypeStruct((rows, width), BF) for _ in range(chips)),
        in_specs=[ANY] * 8,
        out_specs=(ANY,) * (1 + chips),
        scratch_shapes=[
            pltpu.VMEM((chips, group_count, count, width), BF),
            pltpu.VMEM((chips, group_count, count, width), BF),
            pltpu.VMEM((2 * chips, EXP_GRP * units, width), BF),
            pltpu.VMEM((chips, EXP_GRP, width, units), BF),
            pltpu.VMEM((chips, EXP_GRP, width, units), BF),
            pltpu.VMEM((group_count, count, EXP_GRP), F32),
            pltpu.VMEM((EXP_GRP, group_count, count, units), BF),
            pltpu.VMEM((EXP_GRP, group_count, count, units), BF),
            pltpu.VMEM((rows, 2 * EXP_GRP * units), BF),
            pltpu.VMEM((chips, rows, width), BF),
            sems((chips,)), sems((chips,)), sems((2 * chips,)), sems((chips,)), sems((chips,)), sems((3,)),
            sems((chips,)), sems((1,)),
        ],
        compiler_params=params(),
        cost_estimate=COST,
        name="first_pass",
    )(own, other, w_down, w_gate, w_up, lanes, saved_gate, saved_up)
    return results[0], list(results[1:])


def own_kernel(grads_ref, w_gate_ref, w_up_ref, *refs):
    chips = len(refs) - 11
    other_refs, out_ref, refs = refs[:chips], refs[chips], refs[chips + 1 :]
    w_gate, w_up, other, grads, out, w_gate_sems, w_up_sems, other_sems, grads_sems, out_sems = refs
    group_count, _, count, width = out_ref.shape
    order = block_orders(chips)[0]
    arriving = begin(copies_of([(grads_ref, grads)], grads_sems))
    stream = Stream(
        [
            copies_of([(rows_of(w_gate_ref, order[k], width), w_gate.at[k])], w_gate_sems.at[pl.ds(k, 1)])
            + copies_of([(rows_of(w_up_ref, order[k], width), w_up.at[k])], w_up_sems.at[pl.ds(k, 1)])
            + copies_of([(other_refs[k], other.at[k])], other_sems.at[pl.ds(k, 1)])
            for k in range(chips)
        ],
        depth=2,
    )
    leaving = []
    for k in range(chips):
        stream.use(k)
        if k == 0:
            arriving[0].wait()
        part = weights_times(grads[...], w_gate[k], w_up[k]) + other[k].astype(F32)
        out[k] = part.astype(BF).reshape(group_count, count, width)
        leaving += begin(copies_of([(out.at[k], out_ref.at[:, k])], out_sems.at[pl.ds(k, 1)]))
    for copy in leaving:
        copy.wait()


def own_pass(grads, w_gate, w_up, others, group_count):
    rows, width = others[0].shape
    chips = len(others)
    count = rows // group_count
    units = w_gate.shape[2]
    sems = pltpu.SemaphoreType.DMA
    return pl.pallas_call(
        own_kernel,
        out_shape=jax.ShapeDtypeStruct((group_count, chips, count, width), BF),
        in_specs=[ANY] * (3 + chips),
        out_specs=ANY,
        scratch_shapes=[
            pltpu.VMEM((chips, EXP_GRP, width, units), BF),
            pltpu.VMEM((chips, EXP_GRP, width, units), BF),
            pltpu.VMEM((chips, rows, width), BF),
            pltpu.VMEM((rows, grads.shape[1]), BF),
            pltpu.VMEM((chips, group_count, count, width), BF),
            sems((chips,)), sems((chips,)), sems((chips,)), sems((1,)), sems((chips,)),
        ],
        compiler_params=params(),
        cost_estimate=COST,
        name="own_pass",
    )(grads, w_gate, w_up, *others)


def collect_kernel(*refs):
    count = len(Z_FIRST)
    tables, arrived, outs = refs[:count], refs[count : 2 * count], refs[2 * count :]
    group_count, slots, tok_rows = tables[0].shape
    width = arrived[0].shape[-1]
    for z, out in enumerate(outs):
        total = jnp.zeros((tok_rows, width), F32)
        for table, rows in zip(tables, arrived):
            total = total + lax.dot_general(
                table[...].reshape(group_count * slots, tok_rows),
                rows[:, z].reshape(group_count * slots, width),
                TN,
                preferred_element_type=F32,
            )
        out[...] = total.astype(out.dtype)


def collect(tables, arrived):
    group_count, slots, tok_rows = tables[0].shape
    width = arrived[0].shape[-1]
    return pl.pallas_call(
        collect_kernel,
        out_shape=tuple(
            jax.ShapeDtypeStruct((tok_rows, width), F32 if z == 0 else BF) for z in range(len(Z_OFFSETS))
        ),
        compiler_params=params(16 * 1024 * 1024),
        cost_estimate=COST,
        name="collect",
    )(*tables, *arrived)


def finish_kernel(table_ref, rows_ref, own_ref, a_ref, b_ref, c_ref, out_ref):
    group_count, slots, tok_rows = table_ref.shape
    width = rows_ref.shape[-1]
    total = lax.dot_general(
        table_ref[...].reshape(group_count * slots, tok_rows),
        rows_ref[...].reshape(group_count * slots, width),
        TN,
        preferred_element_type=F32,
    )
    total = total + own_ref[...]
    for ref in (a_ref, b_ref, c_ref):
        total = total + ref[...].astype(F32)
    out_ref[...] = total.astype(BF)


def finish(table, rows, own, others):
    tok_rows, width = own.shape
    return pl.pallas_call(
        finish_kernel,
        out_shape=jax.ShapeDtypeStruct((tok_rows, width), BF),
        compiler_params=params(16 * 1024 * 1024),
        cost_estimate=COST,
        name="finish",
    )(table, rows, own, *others)


def on_device(
    grad_out, combine_weight, token_groups, expert_pick, saved_gate, saved_up, w_gate, w_up, w_down
):
    group_count = lax.axis_size("group")
    local_count = lax.axis_size("local")
    chips = local_count // 2
    def shift(value, by):
        pairs = [
            (c * 2 + k, ((c + by) % chips) * 2 + k) for c in range(chips) for k in range(2)
        ]
        return lax.ppermute(value, "local", pairs)

    def swap(value):
        return lax.ppermute(value, "local", [(i, i ^ 1) for i in range(local_count)])

    def exchange(value):
        return lax.all_to_all(value, "group", split_axis=0, concat_axis=0, tiled=True)

    units = w_gate.shape[2]
    down = w_down.reshape(EXP_GRP * units, w_down.shape[2])
    gate_slots = saved_gate.reshape(EXP_GRP, group_count, CAP, units)
    up_slots = saved_up.reshape(EXP_GRP, group_count, CAP, units)

    blocks = [grad_out] + [shift(grad_out, -by) for by in Z_OFFSETS[1:]]
    table, first_out = route(token_groups, expert_pick, combine_weight, grad_out, group_count)
    first_count = Z_LAST[1]
    first_in = exchange(first_out)
    lanes = jnp.transpose(first_in[:, first_count : first_count + EXP_GRP, :CAP], (0, 2, 1)).astype(F32)
    width = grad_out.shape[1]
    tables = [table[:, start : start + count] for start, count in Z_FIRST]
    sent = [spread_tokens(t, blocks) for t in tables]
    last_rows = lax.all_gather(
        after(first_in[:, :first_count].reshape(group_count * first_count, width), sent[0]),
        "local",
        axis=0,
        tiled=False,
    )

    own = [exchange(after(sent[0], lanes))]
    own[0], sent[1] = lax.optimization_barrier((own[0], sent[1]))
    other = [swap(own[0])]
    own.append(exchange(sent[1]))

    def first(k):
        grads, away = first_pass(own[k], other[k], down, w_gate, w_up, lanes, gate_slots, up_slots, Z_FIRST[k])
        return grads, [swap(piece) for piece in away]

    grads, others = first(0)
    last_part = last_pass(after(last_rows, grads), down, w_gate, w_up, lanes, gate_slots, up_slots)
    last_part, own[1], grads, *others = lax.optimization_barrier((last_part, own[1], grads, *others))
    last_sum = lax.psum_scatter(last_part, "local", scatter_dimension=0, tiled=False)
    ready = own_pass(grads, w_gate, w_up, others, group_count)
    first_home = exchange(ready)

    other.append(swap(own[1]))
    grads, others = first(1)
    second_home = exchange(after(own_pass(grads, w_gate, w_up, others, group_count), first_home))
    returned = [first_home, second_home]

    last_home = exchange(after(last_sum, second_home).reshape(group_count, first_count, width))
    pieces = collect(tables, returned)
    others = [shift(piece, by) for piece, by in zip(pieces[1:], Z_OFFSETS[1:])]
    return finish(table[:, :first_count], last_home, pieces[0], others)


def solution(mesh):
    placed = (
        P("group", "local"),
        P("group", None),
        P("group", None),
        P("group", None),
        P("group", None, "local"),
        P("group", None, "local"),
        P("group", None, "local"),
        P("group", None, "local"),
        P("group", "local", None),
    )
    return jax.shard_map(
        on_device, mesh=mesh, in_specs=placed, out_specs=P("group", "local"), check_vma=False
    )
```

```python
import functools

import jax
import jax.numpy as jnp
from jax import lax
from jax.experimental import pallas as pl
from jax.experimental.pallas import tpu as pltpu
from jax.sharding import PartitionSpec as P

EXP_GRP = 3
CAP = 64
LANE_ROWS = 8
Z_LAST = (0, 32)
Z_FIRST = ((32, 16), (48, 16))
Z_OFFSETS = (0, -1, 1, 2)
CHIPS = len(Z_OFFSETS)
VMEM = 60 * 1024 * 1024
BF = jnp.bfloat16
F32 = jnp.float32
NT = (((1,), (1,)), ((), ()))
TN = (((0,), (0,)), ((), ()))


def params(limit=VMEM):
    return pltpu.CompilerParams(vmem_limit_bytes=limit)


COST = pl.CostEstimate(flops=1000, bytes_accessed=1000, transcendentals=0)
SLOW = pl.CostEstimate(flops=150_000_000_000, bytes_accessed=1000, transcendentals=0)


def after(value, *earlier):
    return lax.optimization_barrier((value, *earlier))[0]


def routing_kernel(groups_ref, picks_ref, weights_ref, tok_ref, table_ref, out_ref):
    group_count, slots, tok_rows = table_ref.shape
    first = out_ref.shape[1] - LANE_ROWS
    groups = groups_ref[...]
    picks = picks_ref[...]
    weights = weights_ref[...]
    ids = lax.broadcasted_iota(jnp.int32, (group_count, tok_rows), 0)
    member = jnp.zeros((group_count, tok_rows), jnp.bool_)
    for q in range(groups.shape[0]):
        member = member | (ids == groups[q : q + 1, :])
    earlier = lax.broadcasted_iota(jnp.int32, (tok_rows, tok_rows), 0) < lax.broadcasted_iota(
        jnp.int32, (tok_rows, tok_rows), 1
    )
    slot = jnp.dot(
        member.astype(F32).astype(BF), earlier.astype(F32).astype(BF), preferred_element_type=F32
    ).astype(jnp.int32)
    slot = jnp.where(member, slot, -1)
    slot_ids = lax.broadcasted_iota(jnp.int32, (group_count, slots, tok_rows), 1)
    table = (slot[:, None, :] == slot_ids).astype(F32).astype(BF)
    table_ref[...] = table

    shape = (group_count, LANE_ROWS, tok_rows)
    group_ids = lax.broadcasted_iota(jnp.int32, shape, 0)
    expert_ids = lax.broadcasted_iota(jnp.int32, shape, 1)
    spread = jnp.zeros(shape, F32)
    for k in range(picks.shape[0]):
        pick = picks[k : k + 1, :]
        chosen = jnp.zeros_like(pick)
        for q in range(groups.shape[0]):
            inside = (pick >= q * EXP_GRP) & (pick < (q + 1) * EXP_GRP)
            chosen = chosen + jnp.where(inside, groups[q : q + 1, :] * EXP_GRP + pick - q * EXP_GRP, 0)
        hit = group_ids * EXP_GRP + expert_ids == chosen[:, None, :]
        hit = hit & (expert_ids < EXP_GRP)
        spread = spread + jnp.where(hit, weights[k : k + 1, :][:, None, :], 0.0)
    spread = spread.astype(BF)

    width = out_ref.shape[2]
    rows = jnp.dot(
        table[:, :first].reshape(group_count * first, tok_rows), tok_ref[...], preferred_element_type=F32
    ).astype(BF)
    out_ref[:, :first, :] = rows.reshape(group_count, first, width)
    out_ref[:, first:, :] = jnp.zeros((group_count, LANE_ROWS, width), BF)
    for g in range(group_count):
        lanes = lax.dot_general(spread[g], table[g], NT, preferred_element_type=F32)
        out_ref[g, first:, :slots] = lanes.astype(BF)


def route(token_groups, expert_pick, combine_weight, tokens, group_count):
    tok_rows, width = tokens.shape
    first = Z_LAST[1]
    return pl.pallas_call(
        routing_kernel,
        out_shape=(
            jax.ShapeDtypeStruct((group_count, CAP, tok_rows), BF),
            jax.ShapeDtypeStruct((group_count, first + LANE_ROWS, width), BF),
        ),
        compiler_params=params(),
        cost_estimate=COST,
        name="route",
    )(token_groups.T, expert_pick.T, combine_weight.T, tokens)


def spread_kernel(table_ref, t0, t1, t2, t3, out_ref):
    group_count, slots, tok_rows = table_ref.shape
    table = table_ref[...].reshape(group_count * slots, tok_rows)
    for z, tok in enumerate((t0, t1, t2, t3)):
        rows = jnp.dot(table, tok[...], preferred_element_type=F32).astype(BF)
        out_ref[:, z] = rows.reshape(group_count, slots, rows.shape[1])


def spread_tokens(table, tokens):
    group_count, slots, tok_rows = table.shape
    width = tokens[0].shape[1]
    return pl.pallas_call(
        spread_kernel,
        out_shape=jax.ShapeDtypeStruct((group_count, len(tokens), slots, width), BF),
        compiler_params=params(),
        cost_estimate=COST,
        name="spread",
    )(table, *tokens)


def write_grads(hidden, lane_ref, gate_ref, up_ref, out_ref):
    rows = hidden.shape[0]
    units = gate_ref.shape[-1]
    lanes = lane_ref[...].reshape(rows, EXP_GRP)
    for j in range(EXP_GRP):
        scaled = hidden[:, j * units : (j + 1) * units] * lanes[:, j : j + 1]
        p = gate_ref[j].reshape(rows, units).astype(F32)
        q = up_ref[j].reshape(rows, units).astype(F32)
        sg = 1.0 / (1.0 + jnp.exp(-p))
        gate = scaled * q * sg * (1.0 + p * (1.0 - sg))
        up = scaled * p * sg
        out_ref[:, j * units : (j + 1) * units] = gate.astype(BF)
        out_ref[:, (EXP_GRP + j) * units : (EXP_GRP + j + 1) * units] = up.astype(BF)


ANY = pl.BlockSpec(memory_space=pl.ANY)


def block_orders(chips):
    place = lax.axis_index("local")
    z, core = lax.div(place, 2), lax.rem(place, 2)
    starts = [lax.rem(z + by + chips, chips) * 2 for by in Z_OFFSETS]
    return [start + core for start in starts], [start + 1 - core for start in starts]


def columns_of(ref, block, width):
    return ref.at[:, pl.ds(pl.multiple_of(block * width, 128), width)]


def rows_of(ref, block, width):
    return ref.at[:, pl.ds(pl.multiple_of(block * width, 128), width)]


def copies_of(pairs, sems):
    return [pltpu.make_async_copy(src, dst, sems.at[i]) for i, (src, dst) in enumerate(pairs)]


def begin(copies):
    for copy in copies:
        copy.start()
    return copies


class Stream:
    def __init__(self, groups, depth=3):
        self.groups, self.depth, self.next = groups, depth, 0
        self.ahead(depth)

    def ahead(self, until):
        while self.next < min(until, len(self.groups)):
            begin(self.groups[self.next])
            self.next += 1

    def use(self, index):
        self.ahead(index + 1 + self.depth)
        for copy in self.groups[index]:
            copy.wait()


def saved_copies(start, count, lane_ref, gate_ref, up_ref, lane, gate, up, sems):
    slots = pl.ds(start, count)
    return copies_of(
        [(lane_ref.at[:, slots], lane), (gate_ref.at[:, :, slots], gate), (up_ref.at[:, :, slots], up)], sems
    )


def weights_times(grads, gate, up):
    columns = jnp.concatenate([gate[j] for j in range(EXP_GRP)] + [up[j] for j in range(EXP_GRP)], axis=1)
    return lax.dot_general(grads, columns, NT, preferred_element_type=F32)


def hidden_last_kernel(
    x_ref, down_ref, lane_ref, gate_ref, up_ref, out_ref, x, down, lane, gate, up, grads, x_sems, down_sems,
    saved_sems, out_sems,
):
    blocks, _, width = x_ref.shape
    start, count = Z_LAST
    groups = [
        copies_of([(x_ref.at[k], x.at[k])], x_sems.at[pl.ds(k, 1)])
        + copies_of([(columns_of(down_ref, k, width), down.at[k])], down_sems.at[pl.ds(k, 1)])
        for k in range(blocks)
    ]
    groups[-1] += saved_copies(start, count, lane_ref, gate_ref, up_ref, lane, gate, up, saved_sems)
    stream = Stream(groups)
    total = None
    for k in range(blocks):
        stream.use(k)
        part = lax.dot_general(x[k], down[k], NT, preferred_element_type=F32)
        total = part if total is None else total + part
    write_grads(total, lane, gate, up, grads)
    for copy in begin(copies_of([(grads, out_ref)], out_sems)):
        copy.wait()


def hidden_last(rows_in, w_down, lanes, saved_gate, saved_up):
    blocks, rows, width = rows_in.shape
    units = saved_gate.shape[3]
    group_count = lanes.shape[0]
    count = Z_LAST[1]
    sems = pltpu.SemaphoreType.DMA
    return pl.pallas_call(
        hidden_last_kernel,
        out_shape=jax.ShapeDtypeStruct((rows, 2 * EXP_GRP * units), BF),
        in_specs=[ANY] * 5,
        out_specs=ANY,
        scratch_shapes=[
            pltpu.VMEM((blocks, rows, width), BF),
            pltpu.VMEM((blocks, EXP_GRP * units, width), BF),
            pltpu.VMEM((group_count, count, EXP_GRP), F32),
            pltpu.VMEM((EXP_GRP, group_count, count, units), BF),
            pltpu.VMEM((EXP_GRP, group_count, count, units), BF),
            pltpu.VMEM((rows, 2 * EXP_GRP * units), BF),
            sems((blocks,)), sems((blocks,)), sems((3,)), sems((1,)),
        ],
        compiler_params=params(),
        cost_estimate=COST,
        name="hidden_last",
    )(rows_in, w_down, lanes, saved_gate, saved_up)


def back_last_kernel(
    grads_ref, w_gate_ref, w_up_ref, out_ref, grads, w_gate, w_up, out, grads_sems, w_gate_sems, w_up_sems, out_sems
):
    blocks, _, width = out_ref.shape
    turns = out.shape[0]
    arriving = begin(copies_of([(grads_ref, grads)], grads_sems))
    stream = Stream(
        [
            copies_of([(rows_of(w_gate_ref, k, width), w_gate.at[k])], w_gate_sems.at[pl.ds(k, 1)])
            + copies_of([(rows_of(w_up_ref, k, width), w_up.at[k])], w_up_sems.at[pl.ds(k, 1)])
            for k in range(blocks)
        ]
    )
    arriving[0].wait()
    leaving = []
    for k in range(blocks):
        stream.use(k)
        if k >= turns:
            leaving[k - turns].wait()
        out[k % turns] = weights_times(grads[...], w_gate[k], w_up[k]).astype(BF)
        leaving += begin(copies_of([(out.at[k % turns], out_ref.at[k])], out_sems.at[pl.ds(k, 1)]))
    for copy in leaving[-turns:]:
        copy.wait()


def back_last(grads, w_gate, w_up, blocks):
    rows, depth = grads.shape
    width = w_gate.shape[1] // blocks
    units = w_gate.shape[2]
    sems = pltpu.SemaphoreType.DMA
    return pl.pallas_call(
        back_last_kernel,
        out_shape=jax.ShapeDtypeStruct((blocks, rows, width), BF),
        in_specs=[ANY] * 3,
        out_specs=ANY,
        scratch_shapes=[
            pltpu.VMEM((rows, depth), BF),
            pltpu.VMEM((blocks, EXP_GRP, width, units), BF),
            pltpu.VMEM((blocks, EXP_GRP, width, units), BF),
            pltpu.VMEM((3, rows, width), BF),
            sems((1,)), sems((blocks,)), sems((blocks,)), sems((blocks,)),
        ],
        compiler_params=params(),
        cost_estimate=COST,
        name="back_last",
    )(grads, w_gate, w_up)


def first_kernel(
    start, own_ref, other_ref, down_ref, w_gate_ref, w_up_ref, lane_ref, gate_ref, up_ref, *refs
):
    chips, width = own_ref.shape[1], own_ref.shape[3]
    grads_ref, out_refs, refs = refs[0], refs[1 : 1 + chips], refs[1 + chips :]
    own, other, down, w_gate, w_up, lane, gate, up, grads, out = refs[:10]
    own_sems, other_sems, down_sems, w_gate_sems, w_up_sems, saved_sems, out_sems, grads_sems = refs[10:]
    mine, theirs = block_orders(chips)
    order = mine + theirs
    count = own_ref.shape[2]
    rows = own_ref.shape[0] * count
    groups = []
    for k in range(2 * chips):
        src, dst, sems = (own_ref, own, own_sems) if k < chips else (other_ref, other, other_sems)
        groups.append(
            copies_of([(src.at[:, k % chips], dst.at[k % chips])], sems.at[pl.ds(k % chips, 1)])
            + copies_of([(columns_of(down_ref, order[k], width), down.at[k])], down_sems.at[pl.ds(k, 1)])
        )
    groups[-1] += saved_copies(start, count, lane_ref, gate_ref, up_ref, lane, gate, up, saved_sems)
    for k in range(chips):
        block = order[chips + k]
        groups.append(
            copies_of([(rows_of(w_gate_ref, block, width), w_gate.at[k])], w_gate_sems.at[pl.ds(k, 1)])
            + copies_of([(rows_of(w_up_ref, block, width), w_up.at[k])], w_up_sems.at[pl.ds(k, 1)])
        )
    stream = Stream(groups)
    total = None
    for k in range(2 * chips):
        stream.use(k)
        piece = own[k] if k < chips else other[k - chips]
        part = lax.dot_general(piece.reshape(rows, width), down[k], NT, preferred_element_type=F32)
        total = part if total is None else total + part
    write_grads(total, lane, gate, up, grads)
    leaving = begin(copies_of([(grads, grads_ref)], grads_sems))
    for k in range(chips):
        stream.use(2 * chips + k)
        out[k] = weights_times(grads[...], w_gate[k], w_up[k]).astype(BF)
        leaving += begin(copies_of([(out.at[k], out_refs[k])], out_sems.at[pl.ds(k, 1)]))
    for copy in leaving:
        copy.wait()


def first_pass(own, other, w_down, w_gate, w_up, lanes, saved_gate, saved_up, slots):
    start, count = slots
    group_count, chips, _, width = own.shape
    units = w_gate.shape[2]
    rows = group_count * count
    sems = pltpu.SemaphoreType.DMA
    results = pl.pallas_call(
        functools.partial(first_kernel, start),
        out_shape=(jax.ShapeDtypeStruct((rows, 2 * EXP_GRP * units), BF),)
        + tuple(jax.ShapeDtypeStruct((rows, width), BF) for _ in range(chips)),
        in_specs=[ANY] * 8,
        out_specs=(ANY,) * (1 + chips),
        scratch_shapes=[
            pltpu.VMEM((chips, group_count, count, width), BF),
            pltpu.VMEM((chips, group_count, count, width), BF),
            pltpu.VMEM((2 * chips, EXP_GRP * units, width), BF),
            pltpu.VMEM((chips, EXP_GRP, width, units), BF),
            pltpu.VMEM((chips, EXP_GRP, width, units), BF),
            pltpu.VMEM((group_count, count, EXP_GRP), F32),
            pltpu.VMEM((EXP_GRP, group_count, count, units), BF),
            pltpu.VMEM((EXP_GRP, group_count, count, units), BF),
            pltpu.VMEM((rows, 2 * EXP_GRP * units), BF),
            pltpu.VMEM((chips, rows, width), BF),
            sems((chips,)), sems((chips,)), sems((2 * chips,)), sems((chips,)), sems((chips,)), sems((3,)),
            sems((chips,)), sems((1,)),
        ],
        compiler_params=params(),
        cost_estimate=COST,
        name="first_pass",
    )(own, other, w_down, w_gate, w_up, lanes, saved_gate, saved_up)
    return results[0], list(results[1:])


def own_kernel(grads_ref, w_gate_ref, w_up_ref, *refs):
    chips = len(refs) - 11
    other_refs, out_ref, refs = refs[:chips], refs[chips], refs[chips + 1 :]
    w_gate, w_up, other, grads, out, w_gate_sems, w_up_sems, other_sems, grads_sems, out_sems = refs
    group_count, _, count, width = out_ref.shape
    order = block_orders(chips)[0]
    arriving = begin(copies_of([(grads_ref, grads)], grads_sems))
    stream = Stream(
        [
            copies_of([(rows_of(w_gate_ref, order[k], width), w_gate.at[k])], w_gate_sems.at[pl.ds(k, 1)])
            + copies_of([(rows_of(w_up_ref, order[k], width), w_up.at[k])], w_up_sems.at[pl.ds(k, 1)])
            + copies_of([(other_refs[k], other.at[k])], other_sems.at[pl.ds(k, 1)])
            for k in range(chips)
        ],
        depth=2,
    )
    leaving = []
    for k in range(chips):
        stream.use(k)
        if k == 0:
            arriving[0].wait()
        part = weights_times(grads[...], w_gate[k], w_up[k]) + other[k].astype(F32)
        out[k] = part.astype(BF).reshape(group_count, count, width)
        leaving += begin(copies_of([(out.at[k], out_ref.at[:, k])], out_sems.at[pl.ds(k, 1)]))
    for copy in leaving:
        copy.wait()


def own_pass(grads, w_gate, w_up, others, group_count):
    rows, width = others[0].shape
    chips = len(others)
    count = rows // group_count
    units = w_gate.shape[2]
    sems = pltpu.SemaphoreType.DMA
    return pl.pallas_call(
        own_kernel,
        out_shape=jax.ShapeDtypeStruct((group_count, chips, count, width), BF),
        in_specs=[ANY] * (3 + chips),
        out_specs=ANY,
        scratch_shapes=[
            pltpu.VMEM((chips, EXP_GRP, width, units), BF),
            pltpu.VMEM((chips, EXP_GRP, width, units), BF),
            pltpu.VMEM((chips, rows, width), BF),
            pltpu.VMEM((rows, grads.shape[1]), BF),
            pltpu.VMEM((chips, group_count, count, width), BF),
            sems((chips,)), sems((chips,)), sems((chips,)), sems((1,)), sems((chips,)),
        ],
        compiler_params=params(),
        cost_estimate=COST,
        name="own_pass",
    )(grads, w_gate, w_up, *others)


def cut_kernel(table_ref, *out_refs):
    for (start, count), out_ref in zip((Z_LAST, *Z_FIRST), out_refs):
        out_ref[...] = table_ref[:, start : start + count]


def cut(table):
    group_count, _, tok_rows = table.shape
    return pl.pallas_call(
        cut_kernel,
        out_shape=tuple(
            jax.ShapeDtypeStruct((group_count, count, tok_rows), BF) for _, count in (Z_LAST, *Z_FIRST)
        ),
        compiler_params=params(16 * 1024 * 1024),
        cost_estimate=SLOW,
        name="cut",
    )(table)


def collect_kernel(*refs):
    count = len(Z_FIRST)
    tables, arrived, outs = refs[:count], refs[count : 2 * count], refs[2 * count :]
    group_count, slots, tok_rows = tables[0].shape
    width = arrived[0].shape[-1]
    for z, out in enumerate(outs):
        total = jnp.zeros((tok_rows, width), F32)
        for table, rows in zip(tables, arrived):
            total = total + lax.dot_general(
                table[...].reshape(group_count * slots, tok_rows),
                rows[:, z].reshape(group_count * slots, width),
                TN,
                preferred_element_type=F32,
            )
        out[...] = total.astype(out.dtype)


def collect(tables, arrived):
    group_count, slots, tok_rows = tables[0].shape
    width = arrived[0].shape[-1]
    return pl.pallas_call(
        collect_kernel,
        out_shape=tuple(
            jax.ShapeDtypeStruct((tok_rows, width), F32 if z == 0 else BF) for z in range(len(Z_OFFSETS))
        ),
        compiler_params=params(16 * 1024 * 1024),
        cost_estimate=COST,
        name="collect",
    )(*tables, *arrived)


def finish_kernel(table_ref, rows_ref, own_ref, a_ref, b_ref, c_ref, out_ref):
    group_count, slots, tok_rows = table_ref.shape
    width = rows_ref.shape[-1]
    total = lax.dot_general(
        table_ref[...].reshape(group_count * slots, tok_rows),
        rows_ref[...].reshape(group_count * slots, width),
        TN,
        preferred_element_type=F32,
    )
    total = total + own_ref[...]
    for ref in (a_ref, b_ref, c_ref):
        total = total + ref[...].astype(F32)
    out_ref[...] = total.astype(BF)


def finish(table, rows, own, others):
    tok_rows, width = own.shape
    return pl.pallas_call(
        finish_kernel,
        out_shape=jax.ShapeDtypeStruct((tok_rows, width), BF),
        compiler_params=params(16 * 1024 * 1024),
        cost_estimate=COST,
        name="finish",
    )(table, rows, own, *others)


def on_device(
    grad_out, combine_weight, token_groups, expert_pick, saved_gate, saved_up, w_gate, w_up, w_down
):
    group_count = lax.axis_size("group")
    local_count = lax.axis_size("local")
    chips = local_count // 2
    def shift(value, by):
        pairs = [
            (c * 2 + k, ((c + by) % chips) * 2 + k) for c in range(chips) for k in range(2)
        ]
        return lax.ppermute(value, "local", pairs)

    def swap(value):
        return lax.ppermute(value, "local", [(i, i ^ 1) for i in range(local_count)])

    def exchange(value):
        return lax.all_to_all(value, "group", split_axis=0, concat_axis=0, tiled=True)

    units = w_gate.shape[2]
    down = w_down.reshape(EXP_GRP * units, w_down.shape[2])
    gate_slots = saved_gate.reshape(EXP_GRP, group_count, CAP, units)
    up_slots = saved_up.reshape(EXP_GRP, group_count, CAP, units)

    blocks = [grad_out] + [shift(grad_out, -by) for by in Z_OFFSETS[1:]]
    table, first_out = route(token_groups, expert_pick, combine_weight, grad_out, group_count)
    first_count = Z_LAST[1]
    first_in = exchange(first_out)
    lanes = jnp.transpose(first_in[:, first_count : first_count + EXP_GRP, :CAP], (0, 2, 1)).astype(F32)
    width = grad_out.shape[1]
    tables = [table[:, start : start + count] for start, count in Z_FIRST]
    sent = [spread_tokens(t, blocks) for t in tables]
    last_rows = lax.all_gather(
        after(first_in[:, :first_count].reshape(group_count * first_count, width), sent[0]),
        "local",
        axis=0,
        tiled=False,
    )

    own = [exchange(after(sent[0], first_in))]
    own[0], sent[1], lanes = lax.optimization_barrier((own[0], sent[1], lanes))
    other = [swap(own[0])]
    own.append(exchange(sent[1]))

    def first(k):
        grads, away = first_pass(own[k], other[k], down, w_gate, w_up, lanes, gate_slots, up_slots, Z_FIRST[k])
        return grads, [swap(piece) for piece in away]

    grads, others = first(0)
    last_grads = hidden_last(after(last_rows, grads), down, lanes, gate_slots, up_slots)
    last_grads, grads, *others = lax.optimization_barrier((last_grads, grads, *others))
    ready = own_pass(grads, w_gate, w_up, others, group_count)
    ready, last_grads, own[1] = lax.optimization_barrier((ready, last_grads, own[1]))
    first_home = exchange(ready)
    last_part = back_last(last_grads, w_gate, w_up, local_count)
    last_sum = lax.psum_scatter(last_part, "local", scatter_dimension=0, tiled=False)

    other.append(swap(own[1]))
    own[1] = after(own[1], last_part)
    grads, others = first(1)
    ready = own_pass(grads, w_gate, w_up, others, group_count)
    ready, first_home, table = lax.optimization_barrier((ready, first_home, table))
    last_table, *tables = cut(table)
    second_home = exchange(after(ready, first_home, last_table))
    returned = [first_home, second_home]

    last_home = exchange(after(last_sum, second_home).reshape(group_count, first_count, width))
    pieces = collect(tables, returned)
    others = [shift(piece, by) for piece, by in zip(pieces[1:], Z_OFFSETS[1:])]
    return finish(last_table, last_home, pieces[0], others)


def solution(mesh):
    placed = (
        P("group", "local"),
        P("group", None),
        P("group", None),
        P("group", None),
        P("group", None, "local"),
        P("group", None, "local"),
        P("group", None, "local"),
        P("group", None, "local"),
        P("group", "local", None),
    )
    return jax.shard_map(
        on_device, mesh=mesh, in_specs=placed, out_specs=P("group", "local"), check_vma=False
    )
```

```python
import functools

import jax
import jax.numpy as jnp
from jax import lax
from jax.experimental import pallas as pl
from jax.experimental.pallas import tpu as pltpu
from jax.sharding import PartitionSpec as P

EXP_GRP = 3
CAP = 64
LANE_ROWS = 8
Z_LAST = (0, 32)
Z_FIRST = ((32, 16), (48, 16))
Z_OFFSETS = (0, -1, 1, 2)
CHIPS = len(Z_OFFSETS)
VMEM = 60 * 1024 * 1024
BF = jnp.bfloat16
F32 = jnp.float32
NT = (((1,), (1,)), ((), ()))
TN = (((0,), (0,)), ((), ()))


def params(limit=VMEM):
    return pltpu.CompilerParams(vmem_limit_bytes=limit)


COST = pl.CostEstimate(flops=1000, bytes_accessed=1000, transcendentals=0)
SLOW = pl.CostEstimate(flops=127_000_000_000, bytes_accessed=1000, transcendentals=0)


def after(value, *earlier):
    return lax.optimization_barrier((value, *earlier))[0]


def routing_kernel(groups_ref, picks_ref, weights_ref, tok_ref, table_ref, out_ref):
    group_count, slots, tok_rows = table_ref.shape
    first = out_ref.shape[1] - LANE_ROWS
    groups = groups_ref[...]
    picks = picks_ref[...]
    weights = weights_ref[...]
    ids = lax.broadcasted_iota(jnp.int32, (group_count, tok_rows), 0)
    member = jnp.zeros((group_count, tok_rows), jnp.bool_)
    for q in range(groups.shape[0]):
        member = member | (ids == groups[q : q + 1, :])
    earlier = lax.broadcasted_iota(jnp.int32, (tok_rows, tok_rows), 0) < lax.broadcasted_iota(
        jnp.int32, (tok_rows, tok_rows), 1
    )
    slot = jnp.dot(
        member.astype(F32).astype(BF), earlier.astype(F32).astype(BF), preferred_element_type=F32
    ).astype(jnp.int32)
    slot = jnp.where(member, slot, -1)
    slot_ids = lax.broadcasted_iota(jnp.int32, (group_count, slots, tok_rows), 1)
    table = (slot[:, None, :] == slot_ids).astype(F32).astype(BF)
    table_ref[...] = table

    shape = (group_count, LANE_ROWS, tok_rows)
    group_ids = lax.broadcasted_iota(jnp.int32, shape, 0)
    expert_ids = lax.broadcasted_iota(jnp.int32, shape, 1)
    spread = jnp.zeros(shape, F32)
    for k in range(picks.shape[0]):
        pick = picks[k : k + 1, :]
        chosen = jnp.zeros_like(pick)
        for q in range(groups.shape[0]):
            inside = (pick >= q * EXP_GRP) & (pick < (q + 1) * EXP_GRP)
            chosen = chosen + jnp.where(inside, groups[q : q + 1, :] * EXP_GRP + pick - q * EXP_GRP, 0)
        hit = group_ids * EXP_GRP + expert_ids == chosen[:, None, :]
        hit = hit & (expert_ids < EXP_GRP)
        spread = spread + jnp.where(hit, weights[k : k + 1, :][:, None, :], 0.0)
    spread = spread.astype(BF)

    width = out_ref.shape[2]
    rows = jnp.dot(
        table[:, :first].reshape(group_count * first, tok_rows), tok_ref[...], preferred_element_type=F32
    ).astype(BF)
    out_ref[:, :first, :] = rows.reshape(group_count, first, width)
    out_ref[:, first:, :] = jnp.zeros((group_count, LANE_ROWS, width), BF)
    for g in range(group_count):
        lanes = lax.dot_general(spread[g], table[g], NT, preferred_element_type=F32)
        out_ref[g, first:, :slots] = lanes.astype(BF)


def route(token_groups, expert_pick, combine_weight, tokens, group_count):
    tok_rows, width = tokens.shape
    first = Z_LAST[1]
    return pl.pallas_call(
        routing_kernel,
        out_shape=(
            jax.ShapeDtypeStruct((group_count, CAP, tok_rows), BF),
            jax.ShapeDtypeStruct((group_count, first + LANE_ROWS, width), BF),
        ),
        compiler_params=params(),
        cost_estimate=COST,
        name="route",
    )(token_groups.T, expert_pick.T, combine_weight.T, tokens)


def spread_kernel(table_ref, t0, t1, t2, t3, out_ref):
    group_count, slots, tok_rows = table_ref.shape
    table = table_ref[...].reshape(group_count * slots, tok_rows)
    for z, tok in enumerate((t0, t1, t2, t3)):
        rows = jnp.dot(table, tok[...], preferred_element_type=F32).astype(BF)
        out_ref[:, z] = rows.reshape(group_count, slots, rows.shape[1])


def spread_tokens(table, tokens):
    group_count, slots, tok_rows = table.shape
    width = tokens[0].shape[1]
    return pl.pallas_call(
        spread_kernel,
        out_shape=jax.ShapeDtypeStruct((group_count, len(tokens), slots, width), BF),
        compiler_params=params(),
        cost_estimate=COST,
        name="spread",
    )(table, *tokens)


def write_grads(hidden, lane_ref, gate_ref, up_ref, out_ref):
    rows = hidden.shape[0]
    units = gate_ref.shape[-1]
    lanes = lane_ref[...].reshape(rows, EXP_GRP)
    for j in range(EXP_GRP):
        scaled = hidden[:, j * units : (j + 1) * units] * lanes[:, j : j + 1]
        p = gate_ref[j].reshape(rows, units).astype(F32)
        q = up_ref[j].reshape(rows, units).astype(F32)
        sg = 1.0 / (1.0 + jnp.exp(-p))
        gate = scaled * q * sg * (1.0 + p * (1.0 - sg))
        up = scaled * p * sg
        out_ref[:, j * units : (j + 1) * units] = gate.astype(BF)
        out_ref[:, (EXP_GRP + j) * units : (EXP_GRP + j + 1) * units] = up.astype(BF)


ANY = pl.BlockSpec(memory_space=pl.ANY)


def block_orders(chips):
    place = lax.axis_index("local")
    z, core = lax.div(place, 2), lax.rem(place, 2)
    starts = [lax.rem(z + by + chips, chips) * 2 for by in Z_OFFSETS]
    return [start + core for start in starts], [start + 1 - core for start in starts]


def columns_of(ref, block, width):
    return ref.at[:, pl.ds(pl.multiple_of(block * width, 128), width)]


def rows_of(ref, block, width):
    return ref.at[:, pl.ds(pl.multiple_of(block * width, 128), width)]


def copies_of(pairs, sems):
    return [pltpu.make_async_copy(src, dst, sems.at[i]) for i, (src, dst) in enumerate(pairs)]


def begin(copies):
    for copy in copies:
        copy.start()
    return copies


class Stream:
    def __init__(self, groups, depth=3):
        self.groups, self.depth, self.next = groups, depth, 0
        self.ahead(depth)

    def ahead(self, until):
        while self.next < min(until, len(self.groups)):
            begin(self.groups[self.next])
            self.next += 1

    def use(self, index):
        self.ahead(index + 1 + self.depth)
        for copy in self.groups[index]:
            copy.wait()


def saved_copies(start, count, lane_ref, gate_ref, up_ref, lane, gate, up, sems):
    slots = pl.ds(start, count)
    return copies_of(
        [(lane_ref.at[:, slots], lane), (gate_ref.at[:, :, slots], gate), (up_ref.at[:, :, slots], up)], sems
    )


def weights_times(grads, gate, up):
    columns = jnp.concatenate([gate[j] for j in range(EXP_GRP)] + [up[j] for j in range(EXP_GRP)], axis=1)
    return lax.dot_general(grads, columns, NT, preferred_element_type=F32)


def hidden_last_kernel(
    x_ref, down_ref, lane_ref, gate_ref, up_ref, out_ref, x, down, lane, gate, up, grads, x_sems, down_sems,
    saved_sems, out_sems,
):
    blocks, _, width = x_ref.shape
    start, count = Z_LAST
    groups = [
        copies_of([(x_ref.at[k], x.at[k])], x_sems.at[pl.ds(k, 1)])
        + copies_of([(columns_of(down_ref, k, width), down.at[k])], down_sems.at[pl.ds(k, 1)])
        for k in range(blocks)
    ]
    groups[-1] += saved_copies(start, count, lane_ref, gate_ref, up_ref, lane, gate, up, saved_sems)
    stream = Stream(groups)
    total = None
    for k in range(blocks):
        stream.use(k)
        part = lax.dot_general(x[k], down[k], NT, preferred_element_type=F32)
        total = part if total is None else total + part
    write_grads(total, lane, gate, up, grads)
    for copy in begin(copies_of([(grads, out_ref)], out_sems)):
        copy.wait()


def hidden_last(rows_in, w_down, lanes, saved_gate, saved_up):
    blocks, rows, width = rows_in.shape
    units = saved_gate.shape[3]
    group_count = lanes.shape[0]
    count = Z_LAST[1]
    sems = pltpu.SemaphoreType.DMA
    return pl.pallas_call(
        hidden_last_kernel,
        out_shape=jax.ShapeDtypeStruct((rows, 2 * EXP_GRP * units), BF),
        in_specs=[ANY] * 5,
        out_specs=ANY,
        scratch_shapes=[
            pltpu.VMEM((blocks, rows, width), BF),
            pltpu.VMEM((blocks, EXP_GRP * units, width), BF),
            pltpu.VMEM((group_count, count, EXP_GRP), F32),
            pltpu.VMEM((EXP_GRP, group_count, count, units), BF),
            pltpu.VMEM((EXP_GRP, group_count, count, units), BF),
            pltpu.VMEM((rows, 2 * EXP_GRP * units), BF),
            sems((blocks,)), sems((blocks,)), sems((3,)), sems((1,)),
        ],
        compiler_params=params(),
        cost_estimate=COST,
        name="hidden_last",
    )(rows_in, w_down, lanes, saved_gate, saved_up)


def back_last_kernel(
    grads_ref, w_gate_ref, w_up_ref, out_ref, grads, w_gate, w_up, out, grads_sems, w_gate_sems, w_up_sems, out_sems
):
    blocks, _, width = out_ref.shape
    turns = out.shape[0]
    arriving = begin(copies_of([(grads_ref, grads)], grads_sems))
    stream = Stream(
        [
            copies_of([(rows_of(w_gate_ref, k, width), w_gate.at[k])], w_gate_sems.at[pl.ds(k, 1)])
            + copies_of([(rows_of(w_up_ref, k, width), w_up.at[k])], w_up_sems.at[pl.ds(k, 1)])
            for k in range(blocks)
        ]
    )
    arriving[0].wait()
    leaving = []
    for k in range(blocks):
        stream.use(k)
        if k >= turns:
            leaving[k - turns].wait()
        out[k % turns] = weights_times(grads[...], w_gate[k], w_up[k]).astype(BF)
        leaving += begin(copies_of([(out.at[k % turns], out_ref.at[k])], out_sems.at[pl.ds(k, 1)]))
    for copy in leaving[-turns:]:
        copy.wait()


def back_last(grads, w_gate, w_up, blocks):
    rows, depth = grads.shape
    width = w_gate.shape[1] // blocks
    units = w_gate.shape[2]
    sems = pltpu.SemaphoreType.DMA
    return pl.pallas_call(
        back_last_kernel,
        out_shape=jax.ShapeDtypeStruct((blocks, rows, width), BF),
        in_specs=[ANY] * 3,
        out_specs=ANY,
        scratch_shapes=[
            pltpu.VMEM((rows, depth), BF),
            pltpu.VMEM((blocks, EXP_GRP, width, units), BF),
            pltpu.VMEM((blocks, EXP_GRP, width, units), BF),
            pltpu.VMEM((3, rows, width), BF),
            sems((1,)), sems((blocks,)), sems((blocks,)), sems((blocks,)),
        ],
        compiler_params=params(),
        cost_estimate=COST,
        name="back_last",
    )(grads, w_gate, w_up)


def first_kernel(
    start, own_ref, other_ref, down_ref, w_gate_ref, w_up_ref, lane_ref, gate_ref, up_ref, *refs
):
    chips, width = own_ref.shape[1], own_ref.shape[3]
    grads_ref, out_refs, refs = refs[0], refs[1 : 1 + chips], refs[1 + chips :]
    own, other, down, w_gate, w_up, lane, gate, up, grads, out = refs[:10]
    own_sems, other_sems, down_sems, w_gate_sems, w_up_sems, saved_sems, out_sems, grads_sems = refs[10:]
    mine, theirs = block_orders(chips)
    order = mine + theirs
    count = own_ref.shape[2]
    rows = own_ref.shape[0] * count
    groups = []
    for k in range(2 * chips):
        src, dst, sems = (own_ref, own, own_sems) if k < chips else (other_ref, other, other_sems)
        groups.append(
            copies_of([(src.at[:, k % chips], dst.at[k % chips])], sems.at[pl.ds(k % chips, 1)])
            + copies_of([(columns_of(down_ref, order[k], width), down.at[k])], down_sems.at[pl.ds(k, 1)])
        )
    groups[-1] += saved_copies(start, count, lane_ref, gate_ref, up_ref, lane, gate, up, saved_sems)
    for k in range(chips):
        block = order[chips + k]
        groups.append(
            copies_of([(rows_of(w_gate_ref, block, width), w_gate.at[k])], w_gate_sems.at[pl.ds(k, 1)])
            + copies_of([(rows_of(w_up_ref, block, width), w_up.at[k])], w_up_sems.at[pl.ds(k, 1)])
        )
    stream = Stream(groups)
    total = None
    for k in range(2 * chips):
        stream.use(k)
        piece = own[k] if k < chips else other[k - chips]
        part = lax.dot_general(piece.reshape(rows, width), down[k], NT, preferred_element_type=F32)
        total = part if total is None else total + part
    write_grads(total, lane, gate, up, grads)
    leaving = begin(copies_of([(grads, grads_ref)], grads_sems))
    for k in range(chips):
        stream.use(2 * chips + k)
        out[k] = weights_times(grads[...], w_gate[k], w_up[k]).astype(BF)
        leaving += begin(copies_of([(out.at[k], out_refs[k])], out_sems.at[pl.ds(k, 1)]))
    for copy in leaving:
        copy.wait()


def first_pass(own, other, w_down, w_gate, w_up, lanes, saved_gate, saved_up, slots):
    start, count = slots
    group_count, chips, _, width = own.shape
    units = w_gate.shape[2]
    rows = group_count * count
    sems = pltpu.SemaphoreType.DMA
    results = pl.pallas_call(
        functools.partial(first_kernel, start),
        out_shape=(jax.ShapeDtypeStruct((rows, 2 * EXP_GRP * units), BF),)
        + tuple(jax.ShapeDtypeStruct((rows, width), BF) for _ in range(chips)),
        in_specs=[ANY] * 8,
        out_specs=(ANY,) * (1 + chips),
        scratch_shapes=[
            pltpu.VMEM((chips, group_count, count, width), BF),
            pltpu.VMEM((chips, group_count, count, width), BF),
            pltpu.VMEM((2 * chips, EXP_GRP * units, width), BF),
            pltpu.VMEM((chips, EXP_GRP, width, units), BF),
            pltpu.VMEM((chips, EXP_GRP, width, units), BF),
            pltpu.VMEM((group_count, count, EXP_GRP), F32),
            pltpu.VMEM((EXP_GRP, group_count, count, units), BF),
            pltpu.VMEM((EXP_GRP, group_count, count, units), BF),
            pltpu.VMEM((rows, 2 * EXP_GRP * units), BF),
            pltpu.VMEM((chips, rows, width), BF),
            sems((chips,)), sems((chips,)), sems((2 * chips,)), sems((chips,)), sems((chips,)), sems((3,)),
            sems((chips,)), sems((1,)),
        ],
        compiler_params=params(),
        cost_estimate=COST,
        name="first_pass",
    )(own, other, w_down, w_gate, w_up, lanes, saved_gate, saved_up)
    return results[0], list(results[1:])


def own_kernel(grads_ref, w_gate_ref, w_up_ref, *refs):
    chips = len(refs) - 11
    other_refs, out_ref, refs = refs[:chips], refs[chips], refs[chips + 1 :]
    w_gate, w_up, other, grads, out, w_gate_sems, w_up_sems, other_sems, grads_sems, out_sems = refs
    group_count, _, count, width = out_ref.shape
    order = block_orders(chips)[0]
    arriving = begin(copies_of([(grads_ref, grads)], grads_sems))
    stream = Stream(
        [
            copies_of([(rows_of(w_gate_ref, order[k], width), w_gate.at[k])], w_gate_sems.at[pl.ds(k, 1)])
            + copies_of([(rows_of(w_up_ref, order[k], width), w_up.at[k])], w_up_sems.at[pl.ds(k, 1)])
            + copies_of([(other_refs[k], other.at[k])], other_sems.at[pl.ds(k, 1)])
            for k in range(chips)
        ],
        depth=2,
    )
    leaving = []
    for k in range(chips):
        stream.use(k)
        if k == 0:
            arriving[0].wait()
        part = weights_times(grads[...], w_gate[k], w_up[k]) + other[k].astype(F32)
        out[k] = part.astype(BF).reshape(group_count, count, width)
        leaving += begin(copies_of([(out.at[k], out_ref.at[:, k])], out_sems.at[pl.ds(k, 1)]))
    for copy in leaving:
        copy.wait()


def own_pass(grads, w_gate, w_up, others, group_count):
    rows, width = others[0].shape
    chips = len(others)
    count = rows // group_count
    units = w_gate.shape[2]
    sems = pltpu.SemaphoreType.DMA
    return pl.pallas_call(
        own_kernel,
        out_shape=jax.ShapeDtypeStruct((group_count, chips, count, width), BF),
        in_specs=[ANY] * (3 + chips),
        out_specs=ANY,
        scratch_shapes=[
            pltpu.VMEM((chips, EXP_GRP, width, units), BF),
            pltpu.VMEM((chips, EXP_GRP, width, units), BF),
            pltpu.VMEM((chips, rows, width), BF),
            pltpu.VMEM((rows, grads.shape[1]), BF),
            pltpu.VMEM((chips, group_count, count, width), BF),
            sems((chips,)), sems((chips,)), sems((chips,)), sems((1,)), sems((chips,)),
        ],
        compiler_params=params(),
        cost_estimate=COST,
        name="own_pass",
    )(grads, w_gate, w_up, *others)


def cut_kernel(table_ref, *out_refs):
    for (start, count), out_ref in zip((Z_LAST, *Z_FIRST), out_refs):
        out_ref[...] = table_ref[:, start : start + count]


def cut(table):
    group_count, _, tok_rows = table.shape
    return pl.pallas_call(
        cut_kernel,
        out_shape=tuple(
            jax.ShapeDtypeStruct((group_count, count, tok_rows), BF) for _, count in (Z_LAST, *Z_FIRST)
        ),
        compiler_params=params(16 * 1024 * 1024),
        cost_estimate=SLOW,
        name="cut",
    )(table)


def collect_kernel(*refs):
    count = len(Z_FIRST)
    tables, arrived, outs = refs[:count], refs[count : 2 * count], refs[2 * count :]
    group_count, slots, tok_rows = tables[0].shape
    width = arrived[0].shape[-1]
    for z, out in enumerate(outs):
        total = jnp.zeros((tok_rows, width), F32)
        for table, rows in zip(tables, arrived):
            total = total + lax.dot_general(
                table[...].reshape(group_count * slots, tok_rows),
                rows[:, z].reshape(group_count * slots, width),
                TN,
                preferred_element_type=F32,
            )
        out[...] = total.astype(out.dtype)


def collect(tables, arrived):
    group_count, slots, tok_rows = tables[0].shape
    width = arrived[0].shape[-1]
    return pl.pallas_call(
        collect_kernel,
        out_shape=tuple(
            jax.ShapeDtypeStruct((tok_rows, width), F32 if z == 0 else BF) for z in range(len(Z_OFFSETS))
        ),
        compiler_params=params(16 * 1024 * 1024),
        cost_estimate=COST,
        name="collect",
    )(*tables, *arrived)


def finish_kernel(table_ref, rows_ref, own_ref, a_ref, b_ref, c_ref, out_ref):
    group_count, slots, tok_rows = table_ref.shape
    width = rows_ref.shape[-1]
    total = lax.dot_general(
        table_ref[...].reshape(group_count * slots, tok_rows),
        rows_ref[...].reshape(group_count * slots, width),
        TN,
        preferred_element_type=F32,
    )
    total = total + own_ref[...]
    for ref in (a_ref, b_ref, c_ref):
        total = total + ref[...].astype(F32)
    out_ref[...] = total.astype(BF)


def finish(table, rows, own, others):
    tok_rows, width = own.shape
    return pl.pallas_call(
        finish_kernel,
        out_shape=jax.ShapeDtypeStruct((tok_rows, width), BF),
        compiler_params=params(16 * 1024 * 1024),
        cost_estimate=COST,
        name="finish",
    )(table, rows, own, *others)


def on_device(
    grad_out, combine_weight, token_groups, expert_pick, saved_gate, saved_up, w_gate, w_up, w_down
):
    group_count = lax.axis_size("group")
    local_count = lax.axis_size("local")
    chips = local_count // 2
    def shift(value, by):
        pairs = [
            (c * 2 + k, ((c + by) % chips) * 2 + k) for c in range(chips) for k in range(2)
        ]
        return lax.ppermute(value, "local", pairs)

    def swap(value):
        return lax.ppermute(value, "local", [(i, i ^ 1) for i in range(local_count)])

    def exchange(value):
        return lax.all_to_all(value, "group", split_axis=0, concat_axis=0, tiled=True)

    units = w_gate.shape[2]
    down = w_down.reshape(EXP_GRP * units, w_down.shape[2])
    gate_slots = saved_gate.reshape(EXP_GRP, group_count, CAP, units)
    up_slots = saved_up.reshape(EXP_GRP, group_count, CAP, units)

    blocks = [grad_out] + [shift(grad_out, -by) for by in Z_OFFSETS[1:]]
    table, first_out = route(token_groups, expert_pick, combine_weight, grad_out, group_count)
    first_count = Z_LAST[1]
    first_in = exchange(first_out)
    lanes = jnp.transpose(first_in[:, first_count : first_count + EXP_GRP, :CAP], (0, 2, 1)).astype(F32)
    width = grad_out.shape[1]
    tables = [table[:, start : start + count] for start, count in Z_FIRST]
    sent = [spread_tokens(t, blocks) for t in tables]
    last_rows = lax.all_gather(
        after(first_in[:, :first_count].reshape(group_count * first_count, width), sent[0]),
        "local",
        axis=0,
        tiled=False,
    )

    own = [exchange(after(sent[0], first_in))]
    own[0], sent[1], lanes = lax.optimization_barrier((own[0], sent[1], lanes))
    other = [swap(own[0])]
    own.append(exchange(sent[1]))

    def first(k):
        grads, away = first_pass(own[k], other[k], down, w_gate, w_up, lanes, gate_slots, up_slots, Z_FIRST[k])
        return grads, [swap(piece) for piece in away]

    grads, others = first(0)
    last_grads = hidden_last(after(last_rows, grads), down, lanes, gate_slots, up_slots)
    last_grads, grads, *others = lax.optimization_barrier((last_grads, grads, *others))
    ready = own_pass(grads, w_gate, w_up, others, group_count)
    ready, last_grads, own[1] = lax.optimization_barrier((ready, last_grads, own[1]))
    first_home = exchange(ready)
    last_part = back_last(last_grads, w_gate, w_up, local_count)
    last_sum = lax.psum_scatter(last_part, "local", scatter_dimension=0, tiled=False)

    other.append(swap(own[1]))
    own[1] = after(own[1], last_part)
    grads, others = first(1)
    ready = own_pass(grads, w_gate, w_up, others, group_count)
    last_table, *tables = cut(after(table, ready, first_home))
    second_home = exchange(after(ready, first_home, last_table))
    returned = [first_home, second_home]

    last_home = exchange(after(last_sum, second_home).reshape(group_count, first_count, width))
    pieces = collect(tables, returned)
    others = [shift(piece, by) for piece, by in zip(pieces[1:], Z_OFFSETS[1:])]
    return finish(last_table, last_home, pieces[0], others)


def solution(mesh):
    placed = (
        P("group", "local"),
        P("group", None),
        P("group", None),
        P("group", None),
        P("group", None, "local"),
        P("group", None, "local"),
        P("group", None, "local"),
        P("group", None, "local"),
        P("group", "local", None),
    )
    return jax.shard_map(
        on_device, mesh=mesh, in_specs=placed, out_specs=P("group", "local"), check_vma=False
    )
```

```python
import functools

import jax
import jax.numpy as jnp
from jax import lax
from jax.experimental import pallas as pl
from jax.experimental.pallas import tpu as pltpu
from jax.sharding import PartitionSpec as P

EXP_GRP = 3
CAP = 64
LANE_ROWS = 8
Z_LAST = (0, 32)
Z_FIRST = ((32, 16), (48, 16))
Z_OFFSETS = (0, -1, 1, 2)
CHIPS = len(Z_OFFSETS)
VMEM = 60 * 1024 * 1024
BF = jnp.bfloat16
F32 = jnp.float32
NT = (((1,), (1,)), ((), ()))
TN = (((0,), (0,)), ((), ()))


def params(limit=VMEM):
    return pltpu.CompilerParams(vmem_limit_bytes=limit)


COST = pl.CostEstimate(flops=1000, bytes_accessed=1000, transcendentals=0)
SLOW = pl.CostEstimate(flops=127_000_000_000, bytes_accessed=1000, transcendentals=0)


def after(value, *earlier):
    return lax.optimization_barrier((value, *earlier))[0]


def routing_kernel(groups_ref, picks_ref, weights_ref, tok_ref, table_ref, out_ref):
    group_count, slots, tok_rows = table_ref.shape
    first = out_ref.shape[1] - LANE_ROWS
    groups = groups_ref[...]
    picks = picks_ref[...]
    weights = weights_ref[...]
    ids = lax.broadcasted_iota(jnp.int32, (group_count, tok_rows), 0)
    member = jnp.zeros((group_count, tok_rows), jnp.bool_)
    for q in range(groups.shape[0]):
        member = member | (ids == groups[q : q + 1, :])
    earlier = lax.broadcasted_iota(jnp.int32, (tok_rows, tok_rows), 0) < lax.broadcasted_iota(
        jnp.int32, (tok_rows, tok_rows), 1
    )
    slot = jnp.dot(
        member.astype(F32).astype(BF), earlier.astype(F32).astype(BF), preferred_element_type=F32
    ).astype(jnp.int32)
    slot = jnp.where(member, slot, -1)
    slot_ids = lax.broadcasted_iota(jnp.int32, (group_count, slots, tok_rows), 1)
    table = (slot[:, None, :] == slot_ids).astype(F32).astype(BF)
    table_ref[...] = table

    shape = (group_count, LANE_ROWS, tok_rows)
    group_ids = lax.broadcasted_iota(jnp.int32, shape, 0)
    expert_ids = lax.broadcasted_iota(jnp.int32, shape, 1)
    spread = jnp.zeros(shape, F32)
    for k in range(picks.shape[0]):
        pick = picks[k : k + 1, :]
        chosen = jnp.zeros_like(pick)
        for q in range(groups.shape[0]):
            inside = (pick >= q * EXP_GRP) & (pick < (q + 1) * EXP_GRP)
            chosen = chosen + jnp.where(inside, groups[q : q + 1, :] * EXP_GRP + pick - q * EXP_GRP, 0)
        hit = group_ids * EXP_GRP + expert_ids == chosen[:, None, :]
        hit = hit & (expert_ids < EXP_GRP)
        spread = spread + jnp.where(hit, weights[k : k + 1, :][:, None, :], 0.0)
    spread = spread.astype(BF)

    width = out_ref.shape[2]
    rows = jnp.dot(
        table[:, :first].reshape(group_count * first, tok_rows), tok_ref[...], preferred_element_type=F32
    ).astype(BF)
    out_ref[:, :first, :] = rows.reshape(group_count, first, width)
    out_ref[:, first:, :] = jnp.zeros((group_count, LANE_ROWS, width), BF)
    for g in range(group_count):
        lanes = lax.dot_general(spread[g], table[g], NT, preferred_element_type=F32)
        out_ref[g, first:, :slots] = lanes.astype(BF)


def route(token_groups, expert_pick, combine_weight, tokens, group_count):
    tok_rows, width = tokens.shape
    first = Z_LAST[1]
    return pl.pallas_call(
        routing_kernel,
        out_shape=(
            jax.ShapeDtypeStruct((group_count, CAP, tok_rows), BF),
            jax.ShapeDtypeStruct((group_count, first + LANE_ROWS, width), BF),
        ),
        compiler_params=params(),
        cost_estimate=COST,
        name="route",
    )(token_groups.T, expert_pick.T, combine_weight.T, tokens)


def spread_kernel(table_ref, t0, t1, t2, t3, out_ref):
    group_count, slots, tok_rows = table_ref.shape
    table = table_ref[...].reshape(group_count * slots, tok_rows)
    for z, tok in enumerate((t0, t1, t2, t3)):
        rows = jnp.dot(table, tok[...], preferred_element_type=F32).astype(BF)
        out_ref[:, z] = rows.reshape(group_count, slots, rows.shape[1])


def spread_tokens(table, tokens):
    group_count, slots, tok_rows = table.shape
    width = tokens[0].shape[1]
    return pl.pallas_call(
        spread_kernel,
        out_shape=jax.ShapeDtypeStruct((group_count, len(tokens), slots, width), BF),
        compiler_params=params(16 * 1024 * 1024),
        cost_estimate=COST,
        name="spread",
    )(table, *tokens)


def write_grads(hidden, lane_ref, gate_ref, up_ref, out_ref):
    rows = hidden.shape[0]
    units = gate_ref.shape[-1]
    lanes = lane_ref[...].reshape(rows, EXP_GRP)
    for j in range(EXP_GRP):
        scaled = hidden[:, j * units : (j + 1) * units] * lanes[:, j : j + 1]
        p = gate_ref[j].reshape(rows, units).astype(F32)
        q = up_ref[j].reshape(rows, units).astype(F32)
        sg = 1.0 / (1.0 + jnp.exp(-p))
        gate = scaled * q * sg * (1.0 + p * (1.0 - sg))
        up = scaled * p * sg
        out_ref[:, j * units : (j + 1) * units] = gate.astype(BF)
        out_ref[:, (EXP_GRP + j) * units : (EXP_GRP + j + 1) * units] = up.astype(BF)


ANY = pl.BlockSpec(memory_space=pl.ANY)


def block_orders(chips):
    place = lax.axis_index("local")
    z, core = lax.div(place, 2), lax.rem(place, 2)
    starts = [lax.rem(z + by + chips, chips) * 2 for by in Z_OFFSETS]
    return [start + core for start in starts], [start + 1 - core for start in starts]


def columns_of(ref, block, width):
    return ref.at[:, pl.ds(pl.multiple_of(block * width, 128), width)]


def rows_of(ref, block, width):
    return ref.at[:, pl.ds(pl.multiple_of(block * width, 128), width)]


def copies_of(pairs, sems):
    return [pltpu.make_async_copy(src, dst, sems.at[i]) for i, (src, dst) in enumerate(pairs)]


def begin(copies):
    for copy in copies:
        copy.start()
    return copies


class Stream:
    def __init__(self, groups, depth=3):
        self.groups, self.depth, self.next = groups, depth, 0
        self.ahead(depth)

    def ahead(self, until):
        while self.next < min(until, len(self.groups)):
            begin(self.groups[self.next])
            self.next += 1

    def use(self, index):
        self.ahead(index + 1 + self.depth)
        for copy in self.groups[index]:
            copy.wait()


def saved_copies(start, count, lane_ref, gate_ref, up_ref, lane, gate, up, sems):
    slots = pl.ds(start, count)
    return copies_of(
        [(lane_ref.at[:, slots], lane), (gate_ref.at[:, :, slots], gate), (up_ref.at[:, :, slots], up)], sems
    )


def weights_times(grads, gate, up):
    columns = jnp.concatenate([gate[j] for j in range(EXP_GRP)] + [up[j] for j in range(EXP_GRP)], axis=1)
    return lax.dot_general(grads, columns, NT, preferred_element_type=F32)


def hidden_last_kernel(
    x_ref, down_ref, lane_ref, gate_ref, up_ref, out_ref, x, down, lane, gate, up, grads, x_sems, down_sems,
    saved_sems, out_sems,
):
    blocks, _, width = x_ref.shape
    start, count = Z_LAST
    groups = [
        copies_of([(x_ref.at[k], x.at[k])], x_sems.at[pl.ds(k, 1)])
        + copies_of([(columns_of(down_ref, k, width), down.at[k])], down_sems.at[pl.ds(k, 1)])
        for k in range(blocks)
    ]
    groups[-1] += saved_copies(start, count, lane_ref, gate_ref, up_ref, lane, gate, up, saved_sems)
    stream = Stream(groups)
    total = None
    for k in range(blocks):
        stream.use(k)
        part = lax.dot_general(x[k], down[k], NT, preferred_element_type=F32)
        total = part if total is None else total + part
    write_grads(total, lane, gate, up, grads)
    for copy in begin(copies_of([(grads, out_ref)], out_sems)):
        copy.wait()


def hidden_last(rows_in, w_down, lanes, saved_gate, saved_up):
    blocks, rows, width = rows_in.shape
    units = saved_gate.shape[3]
    group_count = lanes.shape[0]
    count = Z_LAST[1]
    sems = pltpu.SemaphoreType.DMA
    return pl.pallas_call(
        hidden_last_kernel,
        out_shape=jax.ShapeDtypeStruct((rows, 2 * EXP_GRP * units), BF),
        in_specs=[ANY] * 5,
        out_specs=ANY,
        scratch_shapes=[
            pltpu.VMEM((blocks, rows, width), BF),
            pltpu.VMEM((blocks, EXP_GRP * units, width), BF),
            pltpu.VMEM((group_count, count, EXP_GRP), F32),
            pltpu.VMEM((EXP_GRP, group_count, count, units), BF),
            pltpu.VMEM((EXP_GRP, group_count, count, units), BF),
            pltpu.VMEM((rows, 2 * EXP_GRP * units), BF),
            sems((blocks,)), sems((blocks,)), sems((3,)), sems((1,)),
        ],
        compiler_params=params(),
        cost_estimate=COST,
        name="hidden_last",
    )(rows_in, w_down, lanes, saved_gate, saved_up)


def back_last_kernel(
    grads_ref, w_gate_ref, w_up_ref, out_ref, grads, w_gate, w_up, out, grads_sems, w_gate_sems, w_up_sems, out_sems
):
    blocks, _, width = out_ref.shape
    turns = out.shape[0]
    arriving = begin(copies_of([(grads_ref, grads)], grads_sems))
    stream = Stream(
        [
            copies_of([(rows_of(w_gate_ref, k, width), w_gate.at[k])], w_gate_sems.at[pl.ds(k, 1)])
            + copies_of([(rows_of(w_up_ref, k, width), w_up.at[k])], w_up_sems.at[pl.ds(k, 1)])
            for k in range(blocks)
        ]
    )
    arriving[0].wait()
    leaving = []
    for k in range(blocks):
        stream.use(k)
        if k >= turns:
            leaving[k - turns].wait()
        out[k % turns] = weights_times(grads[...], w_gate[k], w_up[k]).astype(BF)
        leaving += begin(copies_of([(out.at[k % turns], out_ref.at[k])], out_sems.at[pl.ds(k, 1)]))
    for copy in leaving[-turns:]:
        copy.wait()


def back_last(grads, w_gate, w_up, blocks):
    rows, depth = grads.shape
    width = w_gate.shape[1] // blocks
    units = w_gate.shape[2]
    sems = pltpu.SemaphoreType.DMA
    return pl.pallas_call(
        back_last_kernel,
        out_shape=jax.ShapeDtypeStruct((blocks, rows, width), BF),
        in_specs=[ANY] * 3,
        out_specs=ANY,
        scratch_shapes=[
            pltpu.VMEM((rows, depth), BF),
            pltpu.VMEM((blocks, EXP_GRP, width, units), BF),
            pltpu.VMEM((blocks, EXP_GRP, width, units), BF),
            pltpu.VMEM((3, rows, width), BF),
            sems((1,)), sems((blocks,)), sems((blocks,)), sems((blocks,)),
        ],
        compiler_params=params(),
        cost_estimate=COST,
        name="back_last",
    )(grads, w_gate, w_up)


def first_kernel(
    start, own_ref, other_ref, down_ref, w_gate_ref, w_up_ref, lane_ref, gate_ref, up_ref, *refs
):
    chips, width = own_ref.shape[1], own_ref.shape[3]
    grads_ref, out_refs, refs = refs[0], refs[1 : 1 + chips], refs[1 + chips :]
    own, other, down, w_gate, w_up, lane, gate, up, grads, out = refs[:10]
    own_sems, other_sems, down_sems, w_gate_sems, w_up_sems, saved_sems, out_sems, grads_sems = refs[10:]
    mine, theirs = block_orders(chips)
    order = mine + theirs
    count = own_ref.shape[2]
    rows = own_ref.shape[0] * count
    groups = []
    for k in range(2 * chips):
        src, dst, sems = (own_ref, own, own_sems) if k < chips else (other_ref, other, other_sems)
        groups.append(
            copies_of([(src.at[:, k % chips], dst.at[k % chips])], sems.at[pl.ds(k % chips, 1)])
            + copies_of([(columns_of(down_ref, order[k], width), down.at[k])], down_sems.at[pl.ds(k, 1)])
        )
    groups[-1] += saved_copies(start, count, lane_ref, gate_ref, up_ref, lane, gate, up, saved_sems)
    for k in range(chips):
        block = order[chips + k]
        groups.append(
            copies_of([(rows_of(w_gate_ref, block, width), w_gate.at[k])], w_gate_sems.at[pl.ds(k, 1)])
            + copies_of([(rows_of(w_up_ref, block, width), w_up.at[k])], w_up_sems.at[pl.ds(k, 1)])
        )
    stream = Stream(groups)
    total = None
    for k in range(2 * chips):
        stream.use(k)
        piece = own[k] if k < chips else other[k - chips]
        part = lax.dot_general(piece.reshape(rows, width), down[k], NT, preferred_element_type=F32)
        total = part if total is None else total + part
    write_grads(total, lane, gate, up, grads)
    leaving = begin(copies_of([(grads, grads_ref)], grads_sems))
    for k in range(chips):
        stream.use(2 * chips + k)
        out[k] = weights_times(grads[...], w_gate[k], w_up[k]).astype(BF)
        leaving += begin(copies_of([(out.at[k], out_refs[k])], out_sems.at[pl.ds(k, 1)]))
    for copy in leaving:
        copy.wait()


def first_pass(own, other, w_down, w_gate, w_up, lanes, saved_gate, saved_up, slots):
    start, count = slots
    group_count, chips, _, width = own.shape
    units = w_gate.shape[2]
    rows = group_count * count
    sems = pltpu.SemaphoreType.DMA
    results = pl.pallas_call(
        functools.partial(first_kernel, start),
        out_shape=(jax.ShapeDtypeStruct((rows, 2 * EXP_GRP * units), BF),)
        + tuple(jax.ShapeDtypeStruct((rows, width), BF) for _ in range(chips)),
        in_specs=[ANY] * 8,
        out_specs=(ANY,) * (1 + chips),
        scratch_shapes=[
            pltpu.VMEM((chips, group_count, count, width), BF),
            pltpu.VMEM((chips, group_count, count, width), BF),
            pltpu.VMEM((2 * chips, EXP_GRP * units, width), BF),
            pltpu.VMEM((chips, EXP_GRP, width, units), BF),
            pltpu.VMEM((chips, EXP_GRP, width, units), BF),
            pltpu.VMEM((group_count, count, EXP_GRP), F32),
            pltpu.VMEM((EXP_GRP, group_count, count, units), BF),
            pltpu.VMEM((EXP_GRP, group_count, count, units), BF),
            pltpu.VMEM((rows, 2 * EXP_GRP * units), BF),
            pltpu.VMEM((chips, rows, width), BF),
            sems((chips,)), sems((chips,)), sems((2 * chips,)), sems((chips,)), sems((chips,)), sems((3,)),
            sems((chips,)), sems((1,)),
        ],
        compiler_params=params(),
        cost_estimate=COST,
        name="first_pass",
    )(own, other, w_down, w_gate, w_up, lanes, saved_gate, saved_up)
    return results[0], list(results[1:])


def own_kernel(grads_ref, w_gate_ref, w_up_ref, *refs):
    chips = len(refs) - 11
    other_refs, out_ref, refs = refs[:chips], refs[chips], refs[chips + 1 :]
    w_gate, w_up, other, grads, out, w_gate_sems, w_up_sems, other_sems, grads_sems, out_sems = refs
    group_count, _, count, width = out_ref.shape
    order = block_orders(chips)[0]
    arriving = begin(copies_of([(grads_ref, grads)], grads_sems))
    stream = Stream(
        [
            copies_of([(rows_of(w_gate_ref, order[k], width), w_gate.at[k])], w_gate_sems.at[pl.ds(k, 1)])
            + copies_of([(rows_of(w_up_ref, order[k], width), w_up.at[k])], w_up_sems.at[pl.ds(k, 1)])
            + copies_of([(other_refs[k], other.at[k])], other_sems.at[pl.ds(k, 1)])
            for k in range(chips)
        ],
        depth=2,
    )
    leaving = []
    for k in range(chips):
        stream.use(k)
        if k == 0:
            arriving[0].wait()
        part = weights_times(grads[...], w_gate[k], w_up[k]) + other[k].astype(F32)
        out[k] = part.astype(BF).reshape(group_count, count, width)
        leaving += begin(copies_of([(out.at[k], out_ref.at[:, k])], out_sems.at[pl.ds(k, 1)]))
    for copy in leaving:
        copy.wait()


def own_pass(grads, w_gate, w_up, others, group_count):
    rows, width = others[0].shape
    chips = len(others)
    count = rows // group_count
    units = w_gate.shape[2]
    sems = pltpu.SemaphoreType.DMA
    return pl.pallas_call(
        own_kernel,
        out_shape=jax.ShapeDtypeStruct((group_count, chips, count, width), BF),
        in_specs=[ANY] * (3 + chips),
        out_specs=ANY,
        scratch_shapes=[
            pltpu.VMEM((chips, EXP_GRP, width, units), BF),
            pltpu.VMEM((chips, EXP_GRP, width, units), BF),
            pltpu.VMEM((chips, rows, width), BF),
            pltpu.VMEM((rows, grads.shape[1]), BF),
            pltpu.VMEM((chips, group_count, count, width), BF),
            sems((chips,)), sems((chips,)), sems((chips,)), sems((1,)), sems((chips,)),
        ],
        compiler_params=params(),
        cost_estimate=COST,
        name="own_pass",
    )(grads, w_gate, w_up, *others)


def cut_kernel(table_ref, *out_refs):
    for (start, count), out_ref in zip((Z_LAST, *Z_FIRST), out_refs):
        out_ref[...] = table_ref[:, start : start + count]


def cut(table):
    group_count, _, tok_rows = table.shape
    return pl.pallas_call(
        cut_kernel,
        out_shape=tuple(
            jax.ShapeDtypeStruct((group_count, count, tok_rows), BF) for _, count in (Z_LAST, *Z_FIRST)
        ),
        compiler_params=params(16 * 1024 * 1024),
        cost_estimate=SLOW,
        name="cut",
    )(table)


def collect_kernel(*refs):
    count = len(Z_FIRST)
    tables, arrived, outs = refs[:count], refs[count : 2 * count], refs[2 * count :]
    group_count, slots, tok_rows = tables[0].shape
    width = arrived[0].shape[-1]
    for z, out in enumerate(outs):
        total = jnp.zeros((tok_rows, width), F32)
        for table, rows in zip(tables, arrived):
            total = total + lax.dot_general(
                table[...].reshape(group_count * slots, tok_rows),
                rows[:, z].reshape(group_count * slots, width),
                TN,
                preferred_element_type=F32,
            )
        out[...] = total.astype(out.dtype)


def collect(tables, arrived):
    group_count, slots, tok_rows = tables[0].shape
    width = arrived[0].shape[-1]
    return pl.pallas_call(
        collect_kernel,
        out_shape=tuple(
            jax.ShapeDtypeStruct((tok_rows, width), F32 if z == 0 else BF) for z in range(len(Z_OFFSETS))
        ),
        compiler_params=params(16 * 1024 * 1024),
        cost_estimate=COST,
        name="collect",
    )(*tables, *arrived)


def finish_kernel(table_ref, rows_ref, own_ref, a_ref, b_ref, c_ref, out_ref):
    group_count, slots, tok_rows = table_ref.shape
    width = rows_ref.shape[-1]
    total = lax.dot_general(
        table_ref[...].reshape(group_count * slots, tok_rows),
        rows_ref[...].reshape(group_count * slots, width),
        TN,
        preferred_element_type=F32,
    )
    total = total + own_ref[...]
    for ref in (a_ref, b_ref, c_ref):
        total = total + ref[...].astype(F32)
    out_ref[...] = total.astype(BF)


def finish(table, rows, own, others):
    tok_rows, width = own.shape
    return pl.pallas_call(
        finish_kernel,
        out_shape=jax.ShapeDtypeStruct((tok_rows, width), BF),
        compiler_params=params(16 * 1024 * 1024),
        cost_estimate=COST,
        name="finish",
    )(table, rows, own, *others)


def on_device(
    grad_out, combine_weight, token_groups, expert_pick, saved_gate, saved_up, w_gate, w_up, w_down
):
    group_count = lax.axis_size("group")
    local_count = lax.axis_size("local")
    chips = local_count // 2
    def shift(value, by):
        pairs = [
            (c * 2 + k, ((c + by) % chips) * 2 + k) for c in range(chips) for k in range(2)
        ]
        return lax.ppermute(value, "local", pairs)

    def swap(value):
        return lax.ppermute(value, "local", [(i, i ^ 1) for i in range(local_count)])

    def exchange(value):
        return lax.all_to_all(value, "group", split_axis=0, concat_axis=0, tiled=True)

    units = w_gate.shape[2]
    down = w_down.reshape(EXP_GRP * units, w_down.shape[2])
    gate_slots = saved_gate.reshape(EXP_GRP, group_count, CAP, units)
    up_slots = saved_up.reshape(EXP_GRP, group_count, CAP, units)

    blocks = [grad_out] + [shift(grad_out, -by) for by in Z_OFFSETS[1:]]
    table, first_out = route(token_groups, expert_pick, combine_weight, grad_out, group_count)
    first_count = Z_LAST[1]
    first_in = exchange(first_out)
    lanes = jnp.transpose(first_in[:, first_count : first_count + EXP_GRP, :CAP], (0, 2, 1)).astype(F32)
    width = grad_out.shape[1]
    tables = [table[:, start : start + count] for start, count in Z_FIRST]
    sent = [spread_tokens(t, blocks) for t in tables]
    last_rows = lax.all_gather(
        after(first_in[:, :first_count].reshape(group_count * first_count, width), sent[0]),
        "local",
        axis=0,
        tiled=False,
    )

    own = [exchange(after(sent[0], first_in))]
    own[0], sent[1], lanes = lax.optimization_barrier((own[0], sent[1], lanes))
    other = [swap(own[0])]
    own.append(exchange(sent[1]))

    def first(k):
        grads, away = first_pass(own[k], other[k], down, w_gate, w_up, lanes, gate_slots, up_slots, Z_FIRST[k])
        return grads, [swap(piece) for piece in away]

    grads, others = first(0)
    last_grads = hidden_last(after(last_rows, grads), down, lanes, gate_slots, up_slots)
    last_grads, grads, *others = lax.optimization_barrier((last_grads, grads, *others))
    ready = own_pass(grads, w_gate, w_up, others, group_count)
    ready, last_grads, own[1] = lax.optimization_barrier((ready, last_grads, own[1]))
    first_home = exchange(ready)
    last_part = back_last(last_grads, w_gate, w_up, local_count)
    last_sum = lax.psum_scatter(last_part, "local", scatter_dimension=0, tiled=False)

    other.append(swap(own[1]))
    own[1] = after(own[1], last_part)
    grads, others = first(1)
    ready = own_pass(grads, w_gate, w_up, others, group_count)
    last_table, *tables = cut(after(table, ready, first_home))
    second_home = exchange(after(ready, first_home, last_table))
    returned = [first_home, second_home]

    last_home = exchange(after(last_sum, second_home).reshape(group_count, first_count, width))
    pieces = collect(tables, returned)
    others = [shift(piece, by) for piece, by in zip(pieces[1:], Z_OFFSETS[1:])]
    return finish(last_table, last_home, pieces[0], others)


def solution(mesh):
    placed = (
        P("group", "local"),
        P("group", None),
        P("group", None),
        P("group", None),
        P("group", None, "local"),
        P("group", None, "local"),
        P("group", None, "local"),
        P("group", None, "local"),
        P("group", "local", None),
    )
    return jax.shard_map(
        on_device, mesh=mesh, in_specs=placed, out_specs=P("group", "local"), check_vma=False
    )
```
